256 devices in a mesh: row: 16 (over z, core), col: 4 (over y), depth: 4 (over x).
Axes of the slice: x: 4, y: 4, z: 8, core: 2. Of those that a mesh axis runs over, the one named last changes fastest.
Arguments:
- a_blocks: bfloat16 [2048, 256, 256], P(('row', 'col', 'depth')), may hold values from -0.375 to 0.375
- a_scale: float32 [2048], P(('row', 'col', 'depth')), may hold values from 0.25 to 4
- a_rows: int32 [2048], P(('row', 'col', 'depth')), may hold values from -1 to 127, as said below
- a_cols: int32 [2048], P(('row', 'col', 'depth')), may hold values from 0 to 127, as said below
- b_blocks: bfloat16 [32, 4, 4, 3, 256, 256], P('row', 'col', 'depth'), may hold values from -6 to 6
- b_scale: float32 [32, 4, 4, 3], P('row', 'col', 'depth'), may hold values from 0.25 to 4
- b_cols: int32 [32, 4, 4, 3], P('row', 'col', 'depth'), may hold values from 0 to 127, as said below
- c_rows: int32 [5120], P(('row', 'col', 'depth')), may hold values from 0 to 127, as said below
- c_cols: int32 [5120], P(('row', 'col', 'depth')), may hold values from 0 to 127, as said below
Outputs:
- c_blocks: bfloat16 [5120, 256, 256], P(('row', 'col', 'depth'))
The draws below stay inside these ranges and needn't reach their ends.
Inputs may be any that keep to these rules, and one draw needn't show every extreme that they name: `a_rows`: slots are laid out device by device in mesh order, 8 a device. A device of row index r holds blocks of block rows r * 8 to (r + 1) * 8 - 1; -1 marks an empty slot; on each device the occupied slots come first, no two occupied slots name the same block, and in every draw some device has all 8 slots occupied. `a_cols`: A device of column index c and depth index e holds blocks whose column k has k % 4 == e and (k // 4) % 4 == c, empty slots included. b_cols[g, c, e, t] lies in block columns c * 32 to (c + 1) * 32 - 1, and the 3 entries of one (g, c, e) differ. `c_rows`: slots are laid out device by device in mesh order, 20 a device. A device of row index r holds result blocks of block rows r * 8 to (r + 1) * 8 - 1; no two slots name the same block. `c_cols`: A device of column index c and depth index e holds result blocks of block columns c * 32 + e * 8 and the next 7.
All inputs are finite; a program needn't handle non-finite values.
Results may differ from the reference program's by a relative error of at most 0.0075.
Values may be sent and summed in bfloat16 or wider, within the bound.
A program may use at most 128 MiB of HBM per device.

```python
import math
import jax
import jax.numpy as jnp
from jax import lax

BLOCK = 256
NB = 128
KB = 3
ROWS_DEV = 8
GRID_COLS = 4
LAYERS = 4
A_CAP = 8
C_CAP = 20
A_SLOTS = 2048
KGROUPS = 32
N_ROW = 16
N_COL = 4
N_DEPTH = 4


def device_grid():
    devices = jnp.arange(N_ROW * N_COL * N_DEPTH)
    return (devices // (N_COL * N_DEPTH), devices // N_DEPTH % N_COL, devices % N_DEPTH)


def chosen_places(key, slot_count):
    places = ROWS_DEV * (NB // (N_COL * N_DEPTH))
    key_list = jax.random.split(key, N_ROW * N_COL * N_DEPTH)
    return jax.vmap(lambda sub_key: jax.random.permutation(sub_key, places)[:slot_count])(key_list)


def a_pattern(key):
    spread = NB // (N_COL * N_DEPTH)
    grid_row, grid_col, grid_depth = device_grid()
    device_count = N_ROW * N_COL * N_DEPTH
    chosen = chosen_places(jax.random.fold_in(key, 101), A_CAP)
    occupied = jax.random.randint(jax.random.fold_in(key, 102), (device_count,), max(1, A_CAP // 2), A_CAP + 1)
    fullest = jax.random.randint(jax.random.fold_in(key, 103), (), 0, device_count)
    occupied = jnp.where(jnp.arange(device_count) == fullest, A_CAP, occupied)
    slot_ids = jnp.arange(A_CAP)
    block_rows = grid_row[:, None] * ROWS_DEV + chosen // spread
    block_rows = jnp.where(slot_ids[None, :] < occupied[:, None], block_rows, -1)
    inner_index = chosen % spread * (N_COL * N_DEPTH) + grid_col[:, None] * N_DEPTH + grid_depth[:, None]
    return (block_rows.reshape(-1).astype(jnp.int32), inner_index.reshape(-1).astype(jnp.int32))


def b_pattern(key):
    key = jax.random.fold_in(key, 7)
    panel_width = NB // N_COL
    key_list = jax.random.split(key, KGROUPS * N_COL * N_DEPTH)
    chosen = jax.vmap(lambda sub_key: jax.random.permutation(sub_key, panel_width)[:KB])(key_list)
    chosen = chosen.reshape(KGROUPS, N_COL, N_DEPTH, KB)
    col_base = (jnp.arange(N_COL) * panel_width)[None, :, None, None]
    return (chosen + col_base).astype(jnp.int32)


def c_pattern(key):
    spread = NB // (N_COL * N_DEPTH)
    places = ROWS_DEV * spread
    grid_row, grid_col, grid_depth = device_grid()
    a_row_list, a_col_list = a_pattern(key)
    rows_by_panel = a_row_list.reshape(N_ROW, -1)
    cols_by_panel = a_col_list.reshape(N_ROW, -1)
    b_targets = b_pattern(key)
    key_list = jax.random.split(jax.random.fold_in(key, 201), N_ROW * N_COL * N_DEPTH)
    place_ids = jnp.arange(places)

    def one_device(grid_r, grid_c, grid_e, sub_key):
        rows_here = rows_by_panel[grid_r]
        cols_here = cols_by_panel[grid_r]
        target_cols = b_targets[cols_here // N_DEPTH, grid_c, cols_here % N_DEPTH]
        place_row = grid_r * ROWS_DEV + place_ids // spread
        place_col = grid_c * (NB // N_COL) + grid_e * spread + place_ids % spread
        hits = (place_row[:, None, None] == rows_here[None, :, None]) & (place_col[:, None, None] == target_cols[None])
        counts = jnp.sum(hits.astype(jnp.int32), axis=(1, 2))
        ranks = jax.random.permutation(sub_key, places).astype(jnp.int32)
        scores = counts * places + ranks
        picked = lax.top_k(scores, C_CAP)[1]
        return (place_row[picked], place_col[picked])
    block_rows, block_cols = jax.vmap(one_device)(grid_row, grid_col, grid_depth, key_list)
    return (block_rows.reshape(-1).astype(jnp.int32), block_cols.reshape(-1).astype(jnp.int32))


def draw_a_rows(key, part):
    return a_pattern(key)[0]


def draw_a_cols(key, part):
    return a_pattern(key)[1]


def draw_c_rows(key, part):
    return c_pattern(key)[0]


def draw_c_cols(key, part):
    return c_pattern(key)[1]


def draw_b_cols(key, part):
    return b_pattern(key)


def steps_of(key, shape, pieces, least, top_value):
    def one(position, shards_of):
        heights = jax.random.uniform(jax.random.fold_in(jax.random.fold_in(key, 6), position), (shards_of,), jnp.float32, least / len(pieces), top_value / len(pieces))
        return jnp.repeat(jnp.exp(heights), shape[position] // shards_of).reshape((-1,) + (1,) * (len(shape) - position - 1))

    gain = one(*pieces[0])
    for cut in pieces[1:]:
        gain = gain * one(*cut)
    return gain


def gaussian(key, dims, width, reach, shards=(), held_as=jnp.bfloat16):
    drawn = jax.random.normal(key, dims, jnp.float32) * width
    if len(shards) > 0:
        drawn = steps_of(key, dims, shards, -0.22, 0.18) * drawn
    return jnp.clip(drawn, min=-reach, max=reach).astype(held_as)


def setup_inputs(seed: int = 0) -> dict:
    splits = jax.random.split(jax.random.key(seed), 10)
    return {
        "a_blocks": gaussian(splits[0], (A_SLOTS, BLOCK, BLOCK), BLOCK ** -0.5, 0.375, ((0, 256),)),
        "a_scale": jnp.clip(jnp.exp(math.log(4.0) - 2.7725887 * jax.random.uniform(splits[1], (A_SLOTS,), jnp.float32) ** steps_of(splits[1], (A_SLOTS,), ((0, 256),), -0.2, 0.2)), 0.25, 4.0),
        "a_rows": draw_a_rows(jax.random.fold_in(splits[9], 71), 0),
        "a_cols": draw_a_cols(jax.random.fold_in(splits[9], 71), 0),
        "b_blocks": gaussian(splits[4], (KGROUPS, GRID_COLS, LAYERS, KB, BLOCK, BLOCK), 1.0, 6.0, ((0, 16), (1, 4), (2, 4))),
        "b_scale": jnp.clip(jnp.exp(math.log(4.0) - 2.7725887 * jax.random.uniform(splits[5], (KGROUPS, GRID_COLS, LAYERS, KB), jnp.float32) ** steps_of(splits[5], (KGROUPS, GRID_COLS, LAYERS, KB), ((0, 16), (1, 4), (2, 4)), -0.2, 0.2)), 0.25, 4.0),
        "b_cols": draw_b_cols(jax.random.fold_in(splits[9], 71), 0),
        "c_rows": draw_c_rows(jax.random.fold_in(splits[9], 71), 0),
        "c_cols": draw_c_cols(jax.random.fold_in(splits[9], 71), 0),
    }


def reference(a_blocks, a_scale, a_rows, a_cols, b_blocks, b_scale, b_cols, c_rows, c_cols):
    block_edge = a_blocks.shape[1]
    blocks_grouped = a_blocks.reshape(N_ROW, -1, block_edge, block_edge)
    scale_grouped = a_scale.reshape(N_ROW, -1)
    rows_grouped = a_rows.reshape(N_ROW, -1)
    cols_grouped = a_cols.reshape(N_ROW, -1)
    want_rows_all = c_rows.reshape(N_ROW, N_COL, -1)
    want_cols_all = c_cols.reshape(N_ROW, N_COL, -1)
    slots_out = want_rows_all.shape[2]

    def one_group(flat_index):
        row_index = flat_index // N_COL
        col_index = flat_index % N_COL
        blocks_a = blocks_grouped[row_index].astype(jnp.float32)
        needed_rows = cols_grouped[row_index]
        panel_blocks = jnp.take(b_blocks, col_index, axis=1).reshape(NB, KB, block_edge, block_edge)
        panel_scale = jnp.take(b_scale, col_index, axis=1).reshape(NB, KB)
        panel_cols = jnp.take(b_cols, col_index, axis=1).reshape(NB, KB)
        chosen = panel_blocks[needed_rows].astype(jnp.float32)
        products = jnp.einsum("aij,atjk->atik", blocks_a, chosen, precision=lax.Precision.HIGHEST)
        weights = scale_grouped[row_index][:, None] * panel_scale[needed_rows]
        target_rows = jnp.broadcast_to(rows_grouped[row_index][:, None], weights.shape)
        target_cols = panel_cols[needed_rows]
        want_rows = want_rows_all[row_index, col_index]
        want_cols = want_cols_all[row_index, col_index]
        matches = (want_rows[:, None, None] == target_rows[None]) & (want_cols[:, None, None] == target_cols[None])
        located = jnp.any(matches, axis=0)
        target = jnp.argmax(matches, axis=0).astype(jnp.int32)
        layer_id = (needed_rows % N_DEPTH).astype(jnp.int32)[:, None]
        segment = jnp.where(located, target * N_DEPTH + layer_id, slots_out * N_DEPTH).astype(jnp.int32)
        weighted = products * weights[:, :, None, None]
        slot_sums = jax.ops.segment_sum(weighted.reshape(-1, block_edge, block_edge), segment.reshape(-1), num_segments=slots_out * N_DEPTH + 1)
        layered = slot_sums[:slots_out * N_DEPTH].reshape(slots_out, N_DEPTH, block_edge, block_edge).astype(jnp.bfloat16)
        layered = lax.optimization_barrier(layered).astype(jnp.float32)
        return jnp.sum(layered, axis=1).astype(jnp.bfloat16)

    result = lax.map(one_group, jnp.arange(N_ROW * N_COL))
    return result.reshape(-1, block_edge, block_edge)
```

```python
import functools

import jax
import jax.numpy as jnp
from jax import lax
from jax.experimental import pallas as pl
from jax.experimental.pallas import tpu as pltpu
from jax.sharding import PartitionSpec as P

MESH = pl.DeviceIdType.MESH
LANES = 128
F32 = jnp.float32


def iota(shape, dim):
    return lax.broadcasted_iota(jnp.int32, shape, dim)


def schedule(dims, meta_x, meta_y, meta_z, tab_int, tab_scale):
    n_x, n_y, n_r, a_cap, per, kb, c_cap = dims
    eye = iota((a_cap, LANES), 0) == iota((a_cap, LANES), 1)

    def column(which):
        parts = [
            jnp.sum(jnp.where(eye, meta_y[c, which : which + 1, :], 0.0), axis=1, keepdims=True)
            for c in range(n_y)
        ]
        return jnp.concatenate(parts, axis=0)

    a_scale, a_rows, a_cols = column(0), column(1), column(2)
    n_a = n_y * a_cap
    group = a_cols.astype(jnp.int32) // n_x
    device, inner = group // per, group % per
    lane = iota((n_a, LANES), 1)
    b_scale = jnp.zeros((n_a, LANES), F32)
    b_cols = jnp.zeros((n_a, LANES), F32)
    for d in range(n_r):
        here = device == d
        b_scale = jnp.where(here, meta_z[d, 3:4, :], b_scale)
        b_cols = jnp.where(here, meta_z[d, 4:5, :], b_cols)
    slots, weights, a_ids, b_ids = [], [], [], []
    n_slots = n_x * c_cap
    for t in range(kb):
        pick = lane == inner * kb + t
        col = jnp.sum(jnp.where(pick, b_cols, 0.0), axis=1, keepdims=True)
        scale = jnp.sum(jnp.where(pick, b_scale, 0.0), axis=1, keepdims=True)
        found = jnp.zeros((n_a, LANES), F32)
        for e in range(n_x):
            hit = (a_rows == meta_x[e, 5:6, :]) & (col == meta_x[e, 6:7, :]) & (lane < c_cap)
            found = jnp.where(hit, (lane + (e * c_cap + 1)).astype(F32), found)
        slot = jnp.max(found, axis=1, keepdims=True)
        slots.append(jnp.where(slot > 0, slot - 1, float(n_slots)))
        weights.append(a_scale * scale)
        a_ids.append(iota((n_a, 1), 0).astype(F32))
        b_ids.append((group * kb + t).astype(F32))
    slot = jnp.concatenate(slots, axis=0)
    weight = jnp.concatenate(weights, axis=0)
    a_id = jnp.concatenate(a_ids, axis=0)
    b_id = jnp.concatenate(b_ids, axis=0)
    n_p = kb * n_a
    place, lane = iota((n_p, LANES), 0), iota((n_p, LANES), 1)
    row_slot = jnp.sum(jnp.where(place == lane, slot, 0.0), axis=0, keepdims=True)
    row_slot = jnp.where(lane[:1] < n_p, row_slot, 1e6)
    earlier = (row_slot == slot) & (lane < place)
    before = (row_slot < slot) | earlier
    rank = jnp.sum(jnp.where(before, 1.0, 0.0), axis=1, keepdims=True)
    keep = jnp.where(jnp.sum(jnp.where(earlier, 1.0, 0.0), axis=1, keepdims=True) > 0, 1.0, 0.0)
    mine = rank == lane.astype(F32)

    def ordered(values):
        return jnp.sum(jnp.where(mine, values, 0.0), axis=0, keepdims=True)

    lane_f = lane.astype(F32)
    last = jnp.sum(jnp.where(slot <= lane_f, 1.0, 0.0), axis=0, keepdims=True) - 1.0
    some = jnp.sum(jnp.where(slot == lane_f, 1.0, 0.0), axis=0, keepdims=True)
    last = jnp.where(some > 0, last, float(n_p))
    zero = jnp.zeros((1, LANES), F32)
    table = jnp.concatenate(
        [ordered(a_id), ordered(b_id), last, zero, zero, zero, zero, zero], axis=0
    ).astype(jnp.int32)
    which = iota(table.shape, 0)
    top = jnp.where(which == 0, n_a - 1, jnp.where(which == 1, n_r * per * kb - 1, n_p))
    tab_int[...] = jnp.clip(table, 0, top)
    tab_scale[...] = jnp.concatenate(
        [ordered(weight), ordered(keep), zero, zero, zero, zero, zero, zero], axis=0
    )


def kernel(
    dims, a_hbm, b_hbm, meta, out_hbm, a_all, b_all, meta_x, meta_y, meta_z, tab_int, tab_scale, ids, scales,
    acc, prod, to_right, to_left, from_left, from_right, result,
    local_sem, meta_send, meta_recv, ring_send, ring_recv, core_send, core_recv, a_send, a_recv,
    c_send_r, c_send_l, c_recv_l, c_recv_r, out_sem,
):
    n_x, n_y, n_r, a_cap, per, kb, c_cap = dims
    n_z = n_r // 2
    row, col, dep = lax.axis_index("row"), lax.axis_index("col"), lax.axis_index("depth")
    z, core = row // 2, row % 2

    def at_z(step):
        return (lax.rem(z + step + n_z, n_z) * 2 + core, col, dep)

    def at_y(step):
        return (row, lax.rem(col + step + n_y, n_y), dep)

    def at_x(step):
        return (row, col, lax.rem(dep + step + n_x, n_x))

    sibling = (z * 2 + 1 - core, col, dep)

    barrier = pltpu.get_barrier_semaphore()
    partners = [sibling, at_z(1), at_z(-1)] + [at_y(j) for j in range(1, n_y)] + [at_x(j) for j in range(1, n_x)]
    for partner in partners:
        pl.semaphore_signal(barrier, inc=1, device_id=partner, device_id_type=MESH)
    pl.semaphore_wait(barrier, len(partners))

    sends = []

    def copy(src, dst, send, recv, device):
        return pltpu.make_async_remote_copy(
            src_ref=src, dst_ref=dst, send_sem=send, recv_sem=recv, device_id=device, device_id_type=MESH
        )

    def push(src, dst, send, recv, device):
        made = copy(src, dst, send, recv, device)
        made.start()
        sends.append(made)

    def pulled(dst, send, recv):
        copy(dst, dst, send, recv, sibling).wait_recv()

    count = 0
    meta_waits = []
    for j in range(1, n_y):
        push(meta, meta_y.at[col], meta_send.at[count], meta_recv.at[count], at_y(j))
        meta_waits.append((meta_y.at[lax.rem(col - j + n_y, n_y)], count))
        count += 1
    for j in range(1, n_x):
        push(meta, meta_x.at[dep], meta_send.at[count], meta_recv.at[count], at_x(j))
        meta_waits.append((meta_x.at[lax.rem(dep - j + n_x, n_x)], count))
        count += 1
    push(meta, meta_z.at[row], meta_send.at[count], meta_recv.at[count], sibling)
    meta_waits.append((meta_z.at[z * 2 + 1 - core], count))
    count += 1
    hops_up, hops_down = n_z // 2, (n_z - 1) // 2
    ring_meta = count
    push(meta, meta_z.at[row], meta_send.at[count], meta_recv.at[count], at_z(1))
    push(meta, meta_z.at[row], meta_send.at[count + 1], meta_recv.at[count + 1], at_z(-1))
    count += 2 * hops_up
    core_meta = count

    def b_piece(origin_z, origin_core, half):
        return b_all.at[pl.ds(((origin_z * 2 + origin_core) * per + half) * kb, kb)]

    up, down = at_z(1), at_z(-1)
    half_a = a_cap // 2

    def a_piece(origin, half):
        return a_all.at[pl.ds(origin * a_cap + half * half_a, half_a)]

    def ring_slot(direction, step, half):
        return (direction * hops_up + step) * 2 + half

    for order in range(2):
        h_up, h_down = order, 1 - order
        s_up, s_down = ring_slot(0, 0, h_up), ring_slot(1, 0, h_down)
        push(b_hbm.at[h_up], b_piece(z, core, h_up), ring_send.at[s_up], ring_recv.at[s_up], up)
        push(b_hbm.at[h_down], b_piece(z, core, h_down), ring_send.at[s_down], ring_recv.at[s_down], down)
        push(a_hbm.at[pl.ds(h_up * half_a, half_a)], a_piece(col, h_up), a_send.at[order], a_recv.at[order], at_y(1))
        push(
            a_hbm.at[pl.ds(h_down * half_a, half_a)], a_piece(col, h_down), a_send.at[3 + order],
            a_recv.at[3 + order], at_y(-1),
        )
    for half in range(per):
        push(b_hbm.at[half], b_piece(z, core, half), core_send.at[half], core_recv.at[half], sibling)
    local = [
        pltpu.make_async_copy(a_hbm, a_all.at[pl.ds(col * a_cap, a_cap)], local_sem.at[0]),
        pltpu.make_async_copy(b_hbm.at[0], b_piece(z, core, 0), local_sem.at[1]),
        pltpu.make_async_copy(b_hbm.at[1], b_piece(z, core, 1), local_sem.at[2]),
    ]
    for made in local:
        made.start()
    meta_x[dep] = meta[...]
    meta_y[col] = meta[...]
    meta_z[row] = meta[...]

    def forward_meta(step):
        for direction, hops in ((0, hops_up), (1, hops_down)):
            if step >= hops:
                continue
            origin_z = lax.rem(z - step - 1 + n_z, n_z) if direction == 0 else lax.rem(z + step + 1, n_z)
            here = meta_z.at[origin_z * 2 + core]
            index = ring_meta + 2 * step + direction
            pulled(here, meta_send.at[index], meta_recv.at[index])
            if step + 1 < hops:
                push(here, here, meta_send.at[index + 2], meta_recv.at[index + 2], up if direction == 0 else down)
            push(here, here, meta_send.at[core_meta + 2 * step + direction],
                 meta_recv.at[core_meta + 2 * step + direction], sibling)
            meta_waits.append((meta_z.at[origin_z * 2 + 1 - core], core_meta + 2 * step + direction))

    core_waits = [(b_piece(z, 1 - core, half), half) for half in range(per)]

    def forward_b(step, order):
        for direction in range(2):
            half = order if direction == 0 else 1 - order
            hops = hops_up if order == 0 else hops_down
            if step >= hops:
                continue
            origin_z = lax.rem(z - step - 1 + n_z, n_z) if direction == 0 else lax.rem(z + step + 1, n_z)
            here = b_piece(origin_z, core, half)
            index = ring_slot(direction, step, half)
            pulled(here, ring_send.at[index], ring_recv.at[index])
            if step + 1 < hops:
                index = ring_slot(direction, step + 1, half)
                push(here, here, ring_send.at[index], ring_recv.at[index], up if direction == 0 else down)
            index = per + ring_slot(direction, step, half)
            push(here, here, core_send.at[index], core_recv.at[index], sibling)
            core_waits.append((b_piece(origin_z, 1 - core, half), index))

    def forward_a():
        here = a_piece(lax.rem(col + n_y - 1, n_y), 0)
        pulled(here, a_send.at[0], a_recv.at[0])
        push(here, here, a_send.at[2], a_recv.at[2], at_y(1))
        here = a_piece(lax.rem(col + 1, n_y), 1)
        pulled(here, a_send.at[3], a_recv.at[3])
        push(here, here, a_send.at[5], a_recv.at[5], at_y(-1))

    forward_meta(0)
    forward_b(0, 0)
    forward_a()
    forward_meta(1)
    forward_b(0, 1)
    forward_meta(2)
    forward_b(1, 0)
    forward_meta(3)
    forward_b(1, 1)
    for here, index in meta_waits:
        pulled(here, meta_send.at[index], meta_recv.at[index])
    schedule(dims, meta_x, meta_y, meta_z, tab_int, tab_scale)
    table = [
        pltpu.make_async_copy(tab_int, ids, local_sem.at[3]),
        pltpu.make_async_copy(tab_scale, scales, local_sem.at[4]),
    ]
    for made in table:
        made.start()
    forward_b(2, 0)
    forward_b(2, 1)
    forward_b(3, 0)
    for made in table + local:
        made.wait()
    pulled(a_piece(lax.rem(col + n_y - 1, n_y), 1), a_send.at[1], a_recv.at[1])
    pulled(a_piece(lax.rem(col + 1, n_y), 0), a_send.at[4], a_recv.at[4])
    opposite = lax.rem(col + 2, n_y)
    pulled(a_piece(opposite, 0), a_send.at[2], a_recv.at[2])
    pulled(a_piece(opposite, 1), a_send.at[5], a_recv.at[5])
    for here, index in core_waits:
        pulled(here, core_send.at[index], core_recv.at[index])

    n_p = kb * n_y * a_cap
    acc[...] = jnp.zeros_like(acc)
    prod[n_p] = jnp.zeros(prod.shape[1:], prod.dtype)

    def bounded(index, size):
        return jnp.clip(index, 0, size - 1)

    @pl.loop(0, n_p)
    def _(j):
        left_block = a_all[bounded(ids[0, j], n_y * a_cap)]
        right_block = b_all[bounded(ids[1, j], n_r * per * kb)]
        product = jnp.dot(left_block, right_block, preferred_element_type=F32)
        total = acc[...] * scales[1, j] + product * scales[0, j]
        acc[...] = total
        prod[j] = total.astype(prod.dtype)

    half_c = c_cap // 2
    piece = 2
    steps = half_c // piece
    right, left = at_x(1), at_x(-1)
    d_right, d_left, d_far = right[2], left[2], lax.rem(dep + 2, n_x)

    def own(dest, index):
        return prod[bounded(ids[2, dest * c_cap + index], n_p + 1)]

    def part(refs, stage, k):
        return refs.at[pl.ds(stage * half_c + k * piece, piece)]

    def send_right(stage, k):
        index = stage * steps + k
        return copy(part(to_right, stage, k), part(from_left, stage, k), c_send_r.at[index], c_recv_l.at[index], right)

    def send_left(stage, k):
        index = stage * steps + k
        return copy(part(to_left, stage, k), part(from_right, stage, k), c_send_l.at[index], c_recv_r.at[index], left)

    def wait_left(stage, k):
        here, index = part(from_left, stage, k), stage * steps + k
        copy(here, here, c_send_r.at[index], c_recv_l.at[index], right).wait_recv()

    def wait_right(stage, k):
        here, index = part(from_right, stage, k), stage * steps + k
        copy(here, here, c_send_l.at[index], c_recv_r.at[index], left).wait_recv()

    @pl.loop(0, steps)
    def _(k):
        for i in range(piece):
            to_right[k * piece + i] = own(d_far, k * piece + i)
        send_right(0, k).start()
        for i in range(piece):
            to_left[k * piece + i] = own(d_far, half_c + k * piece + i)
        send_left(0, k).start()

    @pl.loop(0, steps)
    def _(k):
        for i in range(piece):
            to_right[half_c + k * piece + i] = own(d_right, half_c + k * piece + i)
        send_right(1, k).start()
        for i in range(piece):
            to_left[half_c + k * piece + i] = own(d_left, k * piece + i)
        send_left(1, k).start()

    @pl.loop(0, steps)
    def _(k):
        wait_left(0, k)
        for i in range(piece):
            m = k * piece + i
            total = own(d_right, m).astype(F32) + from_left[m].astype(F32)
            to_right[2 * half_c + m] = total.astype(prod.dtype)
        send_right(2, k).start()
        wait_right(0, k)
        for i in range(piece):
            m = k * piece + i
            total = own(d_left, half_c + m).astype(F32) + from_right[m].astype(F32)
            to_left[2 * half_c + m] = total.astype(prod.dtype)
        send_left(2, k).start()

    def write(half, k):
        here = pl.ds(half * half_c + k * piece, piece)
        return pltpu.make_async_copy(result.at[here], out_hbm.at[here], out_sem.at[half * steps + k])

    @pl.loop(0, steps)
    def _(k):
        wait_right(1, k)
        wait_left(2, k)
        for i in range(piece):
            m = k * piece + i
            total = own(dep, m).astype(F32) + from_left[2 * half_c + m].astype(F32)
            result[m] = (total + from_right[half_c + m].astype(F32)).astype(prod.dtype)
        write(0, k).start()
        wait_left(1, k)
        wait_right(2, k)
        for i in range(piece):
            m = k * piece + i
            total = own(dep, half_c + m).astype(F32) + from_right[2 * half_c + m].astype(F32)
            result[half_c + m] = (total + from_left[half_c + m].astype(F32)).astype(prod.dtype)
        write(1, k).start()

    @pl.loop(0, steps)
    def _(k):
        write(0, k).wait()
        write(1, k).wait()
        for stage in range(3):
            send_right(stage, k).wait_send()
            send_left(stage, k).wait_send()

    for made in sends:
        made.wait_send()


def shards(a_blocks, a_scale, a_rows, a_cols, b_blocks, b_scale, b_cols, c_rows, c_cols):
    edge = a_blocks.shape[1]
    a_cap, c_cap = a_blocks.shape[0], c_rows.shape[0]
    per, kb = b_blocks.shape[0], b_blocks.shape[3]
    n_r, n_y, n_x = lax.axis_size("row"), lax.axis_size("col"), lax.axis_size("depth")
    dims = (n_x, n_y, n_r, a_cap, per, kb, c_cap)
    half_c = c_cap // 2
    n_p = kb * n_y * a_cap

    def line(values):
        flat = values.reshape(-1).astype(F32)
        return jnp.pad(flat, (0, LANES - flat.shape[0]))

    meta = jnp.stack([line(v) for v in (a_scale, a_rows, a_cols, b_scale, b_cols, c_rows, c_cols, c_cols)])
    dtype = a_blocks.dtype
    block = (edge, edge)
    dma = pltpu.SemaphoreType.DMA
    n_z = n_r // 2
    n_meta = (n_y - 1) + (n_x - 1) + 1 + 2 * (n_z // 2) + 2 * (n_z // 2)
    n_ring = 2 * (n_z // 2) * 2
    return pl.pallas_call(
        functools.partial(kernel, dims),
        out_shape=jax.ShapeDtypeStruct((c_cap,) + block, dtype),
        in_specs=[
            pl.BlockSpec(memory_space=pl.ANY),
            pl.BlockSpec(memory_space=pl.ANY),
            pl.BlockSpec(memory_space=pltpu.VMEM),
        ],
        out_specs=pl.BlockSpec(memory_space=pl.ANY),
        scratch_shapes=[
            pltpu.VMEM((n_y * a_cap,) + block, dtype),
            pltpu.VMEM((n_r * per * kb,) + block, dtype),
            pltpu.VMEM((n_x, 8, LANES), F32),
            pltpu.VMEM((n_y, 8, LANES), F32),
            pltpu.VMEM((n_r, 8, LANES), F32),
            pltpu.VMEM((8, LANES), jnp.int32),
            pltpu.VMEM((8, LANES), F32),
            pltpu.SMEM((8, LANES), jnp.int32),
            pltpu.SMEM((8, LANES), F32),
            pltpu.VMEM(block, F32),
            pltpu.VMEM((n_p + 1,) + block, dtype),
            pltpu.VMEM((3 * half_c,) + block, dtype),
            pltpu.VMEM((3 * half_c,) + block, dtype),
            pltpu.VMEM((3 * half_c,) + block, dtype),
            pltpu.VMEM((3 * half_c,) + block, dtype),
            pltpu.VMEM((c_cap,) + block, dtype),
            dma((5,)),
            dma((n_meta,)),
            dma((n_meta,)),
            dma((n_ring,)),
            dma((n_ring,)),
            dma((per + n_ring,)),
            dma((per + n_ring,)),
            dma((6,)),
            dma((6,)),
            dma((3 * half_c,)),
            dma((3 * half_c,)),
            dma((3 * half_c,)),
            dma((3 * half_c,)),
            dma((c_cap,)),
        ],
        compiler_params=pltpu.CompilerParams(
            collective_id=0, has_side_effects=True, vmem_limit_bytes=60 * 1024 * 1024
        ),
    )(a_blocks, b_blocks.reshape(per, kb, edge, edge), meta)


def solution(mesh):
    return jax.shard_map(
        shards,
        mesh=mesh,
        in_specs=(
            P(("row", "col", "depth"), None, None),
            P(("row", "col", "depth")),
            P(("row", "col", "depth")),
            P(("row", "col", "depth")),
            P("row", "col", "depth", None, None, None),
            P("row", "col", "depth", None),
            P("row", "col", "depth", None),
            P(("row", "col", "depth")),
            P(("row", "col", "depth")),
        ),
        out_specs=P(("row", "col", "depth"), None, None),
        check_vma=False,
    )
```

```python
import functools

import jax
import jax.numpy as jnp
from jax import lax
from jax.experimental import pallas as pl
from jax.experimental.pallas import tpu as pltpu
from jax.sharding import PartitionSpec as P

MESH = pl.DeviceIdType.MESH
LANES = 128
ROW_KEY = 1024.0
F32 = jnp.float32


def iota(shape, dim):
    return lax.broadcasted_iota(jnp.int32, shape, dim)


def schedule(dims, meta_x, meta_y, meta_z, tab_int, tab_scale):
    n_x, n_y, n_r, a_cap, per, kb, c_cap = dims
    n_c = n_y * a_cap
    n_a = 2 * n_c
    n_g = n_r * per
    eye = iota((a_cap, LANES), 0) == iota((a_cap, LANES), 1)
    lane = iota((n_c, LANES), 1)
    slots, weights, a_ids, b_ids = [], [], [], []
    n_slots = n_x * c_cap
    for kind in range(2):

        def column(which):
            parts = [
                jnp.sum(jnp.where(eye, meta_y[kind, c, which : which + 1, :], 0.0), axis=1, keepdims=True)
                for c in range(n_y)
            ]
            return jnp.concatenate(parts, axis=0)

        a_scale, a_rows, a_cols = column(0), column(1), column(2)
        group = a_cols.astype(jnp.int32) // n_x
        b_scale = jnp.zeros((n_c, LANES), F32)
        b_cols = jnp.zeros((n_c, LANES), F32)
        for g in range(n_g):
            here = group == g
            d, inner = g // per, g % per
            b_scale = jnp.where(here, meta_z[kind, d, 3 + inner : 4 + inner, :], b_scale)
            b_cols = jnp.where(here, meta_z[kind, d, 5 + inner : 6 + inner, :], b_cols)
        for t in range(kb):
            col = jnp.sum(jnp.where(lane == t, b_cols, 0.0), axis=1, keepdims=True)
            scale = jnp.sum(jnp.where(lane == t, b_scale, 0.0), axis=1, keepdims=True)
            key = a_rows * ROW_KEY + col
            found = jnp.zeros((n_c, LANES), F32)
            for e in range(n_x):
                hit = (key == meta_x[e, 7:8, :]) & (lane < c_cap)
                found = jnp.where(hit, (lane + (e * c_cap + 1)).astype(F32), found)
            slot = jnp.max(found, axis=1, keepdims=True)
            slots.append(jnp.where(slot > 0, slot - 1, float(n_slots)))
            weights.append(a_scale * scale)
            a_ids.append((iota((n_c, 1), 0) + kind * n_c).astype(F32))
            b_ids.append(((group + kind * n_g) * kb + t).astype(F32))
    slot = jnp.concatenate(slots, axis=0)
    weight = jnp.concatenate(weights, axis=0)
    a_id = jnp.concatenate(a_ids, axis=0)
    b_id = jnp.concatenate(b_ids, axis=0)
    n_p = kb * n_a
    width = tab_int.shape[1]
    place, lane = iota((n_p, width), 0), iota((n_p, width), 1)
    row_slot = jnp.sum(jnp.where(place == lane, slot, 0.0), axis=0, keepdims=True)
    row_slot = jnp.where(lane[:1] < n_p, row_slot, 1e6)
    earlier = (row_slot == slot) & (lane < place)
    before = (row_slot < slot) | earlier
    rank = jnp.sum(jnp.where(before, 1.0, 0.0), axis=1, keepdims=True)
    keep = jnp.where(jnp.sum(jnp.where(earlier, 1.0, 0.0), axis=1, keepdims=True) > 0, 1.0, 0.0)
    lane_f = lane.astype(F32)
    mine = rank == lane_f

    def ordered(values):
        return jnp.sum(jnp.where(mine, values, 0.0), axis=0, keepdims=True)

    last = jnp.sum(jnp.where(slot <= lane_f, 1.0, 0.0), axis=0, keepdims=True) - 1.0
    some = jnp.sum(jnp.where(slot == lane_f, 1.0, 0.0), axis=0, keepdims=True)
    last = jnp.where(some > 0, last, float(n_p))
    zero = jnp.zeros((1, width), F32)
    table = jnp.concatenate(
        [ordered(a_id), ordered(b_id), last, zero, zero, zero, zero, zero], axis=0
    ).astype(jnp.int32)
    which = iota(table.shape, 0)
    top = jnp.where(which == 0, n_a - 1, jnp.where(which == 1, 2 * n_g * kb - 1, n_p))
    tab_int[...] = jnp.clip(table, 0, top)
    tab_scale[...] = jnp.concatenate(
        [ordered(weight), ordered(keep), zero, zero, zero, zero, zero, zero], axis=0
    )


def kernel(
    dims, a_hbm, b_hbm, a_scale, a_rows, a_cols, b_scale, b_cols, c_rows, c_cols, out_hbm,
    a_all, b_all, meta, meta_x, meta_y, meta_z, tab_int, tab_scale, ids, scales,
    acc, prod, to_mirror, from_mirror, to_pair, result,
    local_sem, meta_send, meta_recv, ring_send, ring_recv, core_send, core_recv, raw_send, raw_recv, a_send, a_recv,
    m_send, m_recv, p_send, p_recv, out_sem,
):
    n_x, n_y, n_r, a_cap, per, kb, c_cap = dims
    n_z = n_r // 2
    n_g = n_r * per
    n_c = n_y * a_cap
    half = result.shape[2]
    row, col, dep = lax.axis_index("row"), lax.axis_index("col"), lax.axis_index("depth")
    z, core = row // 2, row % 2

    def at_z(step):
        return (lax.rem(z + step + n_z, n_z) * 2 + core, col, dep)

    def at_y(step):
        return (row, lax.rem(col + step + n_y, n_y), dep)

    def at_x(step):
        return (row, col, lax.rem(dep + step + n_x, n_x))

    sibling = (z * 2 + 1 - core, col, dep)
    d_pair, d_mirror, d_far = dep + 1 - 2 * (dep % 2), n_x - 1 - dep, lax.rem(dep + 2, n_x)
    pair, mirror = (row, col, d_pair), (row, col, d_mirror)
    side = ((dep + 1) // 2) % 2
    my_cols = pl.ds(pl.multiple_of(side * half, half), half)
    pair_cols = pl.ds(pl.multiple_of((1 - side) * half, half), half)

    meta[...] = jnp.zeros_like(meta)
    meta[0:1, 0:a_cap] = a_scale[...]
    meta[1:2, 0:a_cap] = a_rows[...].astype(F32)
    meta[2:3, 0:a_cap] = a_cols[...].astype(F32)
    meta[3 : 3 + per, 0:kb] = b_scale[...]
    meta[5 : 5 + per, 0:kb] = b_cols[...].astype(F32)
    meta[7:8, 0:c_cap] = c_rows[...].astype(F32) * ROW_KEY + c_cols[...].astype(F32)

    barrier = pltpu.get_barrier_semaphore()
    partners = [sibling, at_z(1), at_z(-1)] + [at_y(j) for j in range(1, n_y)] + [at_x(j) for j in range(1, n_x)]
    for partner in partners:
        pl.semaphore_signal(barrier, inc=1, device_id=partner, device_id_type=MESH)
    pl.semaphore_wait(barrier, len(partners))

    sends = []

    def copy(src, dst, send, recv, device):
        return pltpu.make_async_remote_copy(
            src_ref=src, dst_ref=dst, send_sem=send, recv_sem=recv, device_id=device, device_id_type=MESH
        )

    def push(src, dst, send, recv, device):
        made = copy(src, dst, send, recv, device)
        made.start()
        sends.append(made)

    def pulled(dst, send, recv):
        copy(dst, dst, send, recv, sibling).wait_recv()

    count = 0
    meta_waits = []
    for j in range(1, n_y):
        push(meta, meta_y.at[0, col], meta_send.at[count], meta_recv.at[count], at_y(j))
        meta_waits.append((meta_y.at[0, lax.rem(col - j + n_y, n_y)], count))
        count += 1
    for j in range(1, n_x):
        push(meta, meta_x.at[dep], meta_send.at[count], meta_recv.at[count], at_x(j))
        meta_waits.append((meta_x.at[lax.rem(dep - j + n_x, n_x)], count))
        count += 1
    push(meta, meta_z.at[0, row], meta_send.at[count], meta_recv.at[count], sibling)
    meta_waits.append((meta_z.at[0, z * 2 + 1 - core], count))
    count += 1
    hops_up, hops_down = n_z // 2, (n_z - 1) // 2
    ring_meta = count
    push(meta, meta_z.at[0, row], meta_send.at[count], meta_recv.at[count], at_z(1))
    push(meta, meta_z.at[0, row], meta_send.at[count + 1], meta_recv.at[count + 1], at_z(-1))
    count += 2 * hops_up
    core_meta = count
    count += 2 * hops_up
    pair_meta = count

    up, down = at_z(1), at_z(-1)
    units = [(kind, inner) for kind in range(2) for inner in range(per)]
    n_u = len(units)

    def b_unit(origin_z, origin_core, unit):
        kind, inner = units[unit]
        return b_all.at[pl.ds(((kind * n_r + origin_z * 2 + origin_core) * per + inner) * kb, kb)]

    def a_part(kind, origin, first, size):
        return a_all.at[pl.ds((kind * n_y + origin) * a_cap + first, size)]

    def ring_slot(direction, step, unit):
        return (direction * hops_up + step) * n_u + unit

    def hops(direction, unit):
        return hops_up if units[unit][0] == direction else hops_down

    def send_first(src, unit):
        for direction, device in ((0, up), (1, down)):
            index = ring_slot(direction, 0, unit)
            push(src, b_unit(z, core, unit), ring_send.at[index], ring_recv.at[index], device)
        push(src, b_unit(z, core, unit), core_send.at[unit], core_recv.at[unit], sibling)

    for inner in range(per):
        push(b_hbm.at[inner, :, :, pair_cols], b_unit(z, core, per + inner), raw_send.at[inner], raw_recv.at[inner], pair)
        send_first(b_hbm.at[inner, :, :, my_cols], inner)

    mid = a_cap // 2
    n_ring = a_cap * 3 // 4
    n_part = n_ring // 2
    y_up, y_down = at_y(1), at_y(-1)
    left, right, across = at_y(-1)[1], at_y(1)[1], at_y(2)[1]

    def own_a(first, size, slot, device):
        push(a_hbm.at[pl.ds(first, size)], a_part(0, col, first, size), a_send.at[slot], a_recv.at[slot], device)

    own_a(0, mid, 0, y_up)
    own_a(mid, mid, 3, y_down)

    def raw_a(first, size, slot):
        push(a_hbm.at[pl.ds(first, size)], a_part(1, col, first, size), a_send.at[slot], a_recv.at[slot], pair)

    raw_a(0, n_part, 12)
    own_a(mid, mid, 1, y_up)
    own_a(0, mid, 4, y_down)
    raw_a(n_part, n_part, 13)
    raw_a(n_ring, a_cap - n_ring, 14)
    local = [
        pltpu.make_async_copy(a_hbm, a_part(0, col, 0, a_cap), local_sem.at[0]),
    ]
    for inner in range(per):
        local.append(
            pltpu.make_async_copy(b_hbm.at[inner, :, :, my_cols], b_unit(z, core, inner), local_sem.at[1 + inner])
        )
    for made in local:
        made.start()
    meta_x[dep] = meta[...]
    meta_y[0, col] = meta[...]
    meta_z[0, row] = meta[...]

    def forward_meta(step):
        for direction, limit in ((0, hops_up), (1, hops_down)):
            if step >= limit:
                continue
            origin_z = lax.rem(z - step - 1 + n_z, n_z) if direction == 0 else lax.rem(z + step + 1, n_z)
            here = meta_z.at[0, origin_z * 2 + core]
            index = ring_meta + 2 * step + direction
            pulled(here, meta_send.at[index], meta_recv.at[index])
            if step + 1 < limit:
                push(here, here, meta_send.at[index + 2], meta_recv.at[index + 2], up if direction == 0 else down)
            index = core_meta + 2 * step + direction
            push(here, here, meta_send.at[index], meta_recv.at[index], sibling)
            meta_waits.append((meta_z.at[0, origin_z * 2 + 1 - core], index))

    def pair_tables():
        for here, index in meta_waits:
            pulled(here, meta_send.at[index], meta_recv.at[index])
        push(meta_y.at[0], meta_y.at[1], meta_send.at[pair_meta], meta_recv.at[pair_meta], pair)
        push(meta_z.at[0], meta_z.at[1], meta_send.at[pair_meta + 1], meta_recv.at[pair_meta + 1], pair)

    core_waits = [(b_unit(z, 1 - core, unit), unit) for unit in range(n_u)]

    def forward_raw(inner):
        here = b_unit(z, core, per + inner)
        pulled(here, raw_send.at[inner], raw_recv.at[inner])
        send_first(here, per + inner)

    def forward_b(step, unit):
        for direction in range(2):
            limit = hops(direction, unit)
            if step >= limit:
                continue
            origin_z = lax.rem(z - step - 1 + n_z, n_z) if direction == 0 else lax.rem(z + step + 1, n_z)
            here = b_unit(origin_z, core, unit)
            index = ring_slot(direction, step, unit)
            pulled(here, ring_send.at[index], ring_recv.at[index])
            if step + 1 < limit:
                index = ring_slot(direction, step + 1, unit)
                push(here, here, ring_send.at[index], ring_recv.at[index], up if direction == 0 else down)
            index = n_u + ring_slot(direction, step, unit)
            push(here, here, core_send.at[index], core_recv.at[index], sibling)
            core_waits.append((b_unit(origin_z, 1 - core, unit), index))

    def arrived(kind, origin, first, size, slot):
        here = a_part(kind, origin, first, size)
        pulled(here, a_send.at[slot], a_recv.at[slot])
        return here

    def hand_on(here, slot, device):
        push(here, here, a_send.at[slot], a_recv.at[slot], device)

    def to_pair_a(origin, slot):
        size = a_cap - n_ring
        push(a_part(0, origin, n_ring, size), a_part(1, origin, n_ring, size), a_send.at[slot], a_recv.at[slot], pair)

    forward_meta(0)
    forward_raw(0)
    forward_b(0, 0)
    forward_raw(1)
    forward_b(0, 1)
    forward_meta(1)
    hand_on(arrived(0, left, 0, mid, 0), 2, y_up)
    hand_on(arrived(0, right, mid, mid, 3), 5, y_down)
    to_pair_a(right, 16)
    forward_b(0, 2)
    forward_meta(2)
    here = arrived(1, col, 0, n_part, 12)
    hand_on(here, 6, y_up)
    hand_on(here, 10, y_down)
    forward_b(0, 3)
    forward_meta(3)
    forward_b(1, 0)
    arrived(0, left, mid, mid, 1)
    to_pair_a(left, 15)
    here = arrived(1, col, n_part, n_part, 13)
    hand_on(here, 7, y_up)
    hand_on(here, 9, y_down)
    forward_b(1, 1)
    pair_tables()
    forward_b(1, 2)
    arrived(0, across, mid, mid, 5)
    to_pair_a(across, 17)
    forward_b(1, 3)
    forward_b(2, 0)
    hand_on(arrived(1, left, 0, n_part, 6), 8, y_up)
    forward_b(2, 1)
    hand_on(arrived(1, right, n_part, n_part, 9), 11, y_down)
    forward_b(2, 2)
    pulled(meta_y.at[1], meta_send.at[pair_meta], meta_recv.at[pair_meta])
    pulled(meta_z.at[1], meta_send.at[pair_meta + 1], meta_recv.at[pair_meta + 1])
    schedule(dims, meta_x, meta_y, meta_z, tab_int, tab_scale)
    table = [
        pltpu.make_async_copy(tab_int, ids, local_sem.at[3]),
        pltpu.make_async_copy(tab_scale, scales, local_sem.at[4]),
    ]
    for made in table:
        made.start()
    forward_b(2, 3)
    for unit in range(n_u):
        forward_b(3, unit)
    for made in table + local:
        made.wait()
    arrived(0, right, 0, mid, 4)
    arrived(0, across, 0, mid, 2)
    arrived(1, col, n_ring, a_cap - n_ring, 14)
    arrived(1, left, n_part, n_part, 7)
    arrived(1, right, 0, n_part, 10)
    arrived(1, across, 0, n_part, 8)
    arrived(1, across, n_part, n_part, 11)
    arrived(1, left, n_ring, a_cap - n_ring, 15)
    arrived(1, right, n_ring, a_cap - n_ring, 16)
    arrived(1, across, n_ring, a_cap - n_ring, 17)
    for here, index in core_waits:
        pulled(here, core_send.at[index], core_recv.at[index])

    n_p = kb * 2 * n_c
    acc[...] = jnp.zeros_like(acc)
    prod[n_p] = jnp.zeros(prod.shape[1:], prod.dtype)

    def bounded(index, size):
        return jnp.clip(index, 0, size - 1)

    @pl.loop(0, n_p, unroll=8)
    def _(j):
        left_block = a_all[bounded(ids[0, j], 2 * n_c)]
        right_block = b_all[bounded(ids[1, j], 2 * n_g * kb)]
        product = jnp.dot(left_block, right_block, preferred_element_type=F32)
        total = acc[...] * scales[1, j] + product * scales[0, j]
        acc[...] = total
        prod[j] = total.astype(prod.dtype)

    piece = 4
    steps = c_cap // piece

    def own(dest, index):
        return prod[bounded(ids[2, dest * c_cap + index], n_p + 1)]

    def part(refs, stage, k):
        return refs.at[pl.ds(stage * c_cap + k * piece, piece)]

    def send_mirror(stage, k):
        index = stage * steps + k
        return copy(part(to_mirror, stage, k), part(from_mirror, stage, k), m_send.at[index], m_recv.at[index], mirror)

    def send_pair(k):
        there = out_hbm.at[pl.ds(k * piece, piece), :, my_cols]
        return copy(part(to_pair, 0, k), there, p_send.at[k], p_recv.at[k], pair)

    def write(k):
        return pltpu.make_async_copy(part(result, 0, k), out_hbm.at[pl.ds(k * piece, piece), :, my_cols], out_sem.at[k])

    for stage, dest in ((0, d_far), (1, d_mirror)):

        @pl.loop(0, steps)
        def _(k):
            for i in range(piece):
                to_mirror[stage * c_cap + k * piece + i] = own(dest, k * piece + i)
            send_mirror(stage, k).start()

    def add(dest, stage, m):
        return (own(dest, m).astype(F32) + from_mirror[stage * c_cap + m].astype(F32)).astype(prod.dtype)

    @pl.loop(0, steps)
    def _(k):
        send_mirror(0, k).wait_recv()
        for i in range(piece):
            to_pair[k * piece + i] = add(d_pair, 0, k * piece + i)
        send_pair(k).start()

    @pl.loop(0, steps)
    def _(k):
        send_mirror(1, k).wait_recv()
        for i in range(piece):
            result[k * piece + i] = add(dep, 1, k * piece + i)
        write(k).start()

    @pl.loop(0, steps)
    def _(k):
        write(k).wait()
        here = out_hbm.at[pl.ds(k * piece, piece), :, pair_cols]
        copy(here, here, p_send.at[k], p_recv.at[k], pair).wait_recv()
        send_pair(k).wait_send()
        send_mirror(0, k).wait_send()
        send_mirror(1, k).wait_send()

    for made in sends:
        made.wait_send()


def shards(a_blocks, a_scale, a_rows, a_cols, b_blocks, b_scale, b_cols, c_rows, c_cols):
    edge = a_blocks.shape[1]
    half = edge // 2
    a_cap, c_cap = a_blocks.shape[0], c_rows.shape[0]
    per, kb = b_blocks.shape[0], b_blocks.shape[3]
    n_r, n_y, n_x = lax.axis_size("row"), lax.axis_size("col"), lax.axis_size("depth")
    dims = (n_x, n_y, n_r, a_cap, per, kb, c_cap)
    n_p = kb * n_y * a_cap * 2
    width = -(-n_p // LANES) * LANES
    dtype = a_blocks.dtype
    block, part = (edge, edge), (edge, half)
    dma = pltpu.SemaphoreType.DMA
    hops = n_r // 4
    n_meta = (n_y - 1) + (n_x - 1) + 1 + 4 * hops + 2
    n_ring = 2 * hops * 2 * per
    any_space = pl.BlockSpec(memory_space=pl.ANY)
    vmem = pl.BlockSpec(memory_space=pltpu.VMEM)
    return pl.pallas_call(
        functools.partial(kernel, dims),
        out_shape=jax.ShapeDtypeStruct((c_cap,) + block, dtype),
        in_specs=[any_space, any_space] + [vmem] * 7,
        out_specs=any_space,
        scratch_shapes=[
            pltpu.VMEM((2 * n_y * a_cap,) + block, dtype),
            pltpu.VMEM((2 * n_r * per * kb,) + part, dtype),
            pltpu.VMEM((8, LANES), F32),
            pltpu.VMEM((n_x, 8, LANES), F32),
            pltpu.VMEM((2, n_y, 8, LANES), F32),
            pltpu.VMEM((2, n_r, 8, LANES), F32),
            pltpu.VMEM((8, width), jnp.int32),
            pltpu.VMEM((8, width), F32),
            pltpu.SMEM((8, width), jnp.int32),
            pltpu.SMEM((8, width), F32),
            pltpu.VMEM(part, F32),
            pltpu.VMEM((n_p + 1,) + part, dtype),
            pltpu.VMEM((2 * c_cap,) + part, dtype),
            pltpu.VMEM((2 * c_cap,) + part, dtype),
            pltpu.VMEM((c_cap,) + part, dtype),
            pltpu.VMEM((c_cap,) + part, dtype),
            dma((5,)),
            dma((n_meta,)),
            dma((n_meta,)),
            dma((n_ring,)),
            dma((n_ring,)),
            dma((2 * per + n_ring,)),
            dma((2 * per + n_ring,)),
            dma((per,)),
            dma((per,)),
            dma((18,)),
            dma((18,)),
            dma((2 * c_cap,)),
            dma((2 * c_cap,)),
            dma((c_cap,)),
            dma((c_cap,)),
            dma((c_cap,)),
        ],
        compiler_params=pltpu.CompilerParams(
            collective_id=0, has_side_effects=True, vmem_limit_bytes=60 * 1024 * 1024
        ),
    )(
        a_blocks,
        b_blocks.reshape(per, kb, edge, edge),
        a_scale.reshape(1, a_cap),
        a_rows.reshape(1, a_cap),
        a_cols.reshape(1, a_cap),
        b_scale.reshape(per, kb),
        b_cols.reshape(per, kb),
        c_rows.reshape(1, c_cap),
        c_cols.reshape(1, c_cap),
    )


def solution(mesh):
    return jax.shard_map(
        shards,
        mesh=mesh,
        in_specs=(
            P(("row", "col", "depth"), None, None),
            P(("row", "col", "depth")),
            P(("row", "col", "depth")),
            P(("row", "col", "depth")),
            P("row", "col", "depth", None, None, None),
            P("row", "col", "depth", None),
            P("row", "col", "depth", None),
            P(("row", "col", "depth")),
            P(("row", "col", "depth")),
        ),
        out_specs=P(("row", "col", "depth"), None, None),
        check_vma=False,
    )
```

```python
import functools

import jax
import jax.numpy as jnp
from jax import lax
from jax.experimental import pallas as pl
from jax.experimental.pallas import tpu as pltpu
from jax.sharding import PartitionSpec as P

MESH = pl.DeviceIdType.MESH
LANES = 128
ROW_KEY = 1024.0
F32 = jnp.float32


def iota(shape, dim):
    return lax.broadcasted_iota(jnp.int32, shape, dim)


def schedule(dims, kind, meta_x, meta_y, meta_z, tab_int, tab_scale):
    n_x, n_y, n_r, a_cap, per, kb, c_cap = dims
    n_a = n_y * a_cap
    n_g = n_r * per
    n_slots = n_x * c_cap
    eye = iota((a_cap, LANES), 0) == iota((a_cap, LANES), 1)
    lane = iota((n_a, LANES), 1)

    def column(which):
        parts = [
            jnp.sum(jnp.where(eye, meta_y[kind, c, which : which + 1, :], 0.0), axis=1, keepdims=True)
            for c in range(n_y)
        ]
        return jnp.concatenate(parts, axis=0)

    a_scale, a_rows, a_cols = column(0), column(1), column(2)
    group = a_cols.astype(jnp.int32) // n_x
    b_scale = jnp.zeros((n_a, LANES), F32)
    b_cols = jnp.zeros((n_a, LANES), F32)
    for g in range(n_g):
        here = group == g
        d, inner = g // per, g % per
        b_scale = jnp.where(here, meta_z[kind, d, 3 + inner : 4 + inner, :], b_scale)
        b_cols = jnp.where(here, meta_z[kind, d, 5 + inner : 6 + inner, :], b_cols)
    slots, weights, b_ids = [], [], []
    for t in range(kb):
        col = jnp.sum(jnp.where(lane == t, b_cols, 0.0), axis=1, keepdims=True)
        scale = jnp.sum(jnp.where(lane == t, b_scale, 0.0), axis=1, keepdims=True)
        key = a_rows * ROW_KEY + col
        found = jnp.zeros((n_a, LANES), F32)
        for e in range(n_x):
            hit = (key == meta_x[e, 7:8, :]) & (lane < c_cap)
            found = jnp.where(hit, (lane + (e * c_cap + 1)).astype(F32), found)
        slot = jnp.max(found, axis=1, keepdims=True)
        slots.append(jnp.where(slot > 0, slot - 1, float(n_slots)))
        weights.append(a_scale * scale)
        b_ids.append((group * kb + t).astype(F32))
    slot, weight = jnp.concatenate(slots, axis=0), jnp.concatenate(weights, axis=0)
    a_id = jnp.concatenate([iota((n_a, 1), 0).astype(F32)] * kb, axis=0)
    b_id = jnp.concatenate(b_ids, axis=0)
    n_p = kb * n_a
    width = tab_int.shape[1]
    place, lane = iota((n_p, width), 0), iota((n_p, width), 1)
    row_slot = jnp.sum(jnp.where(place == lane, slot, 0.0), axis=0, keepdims=True)
    row_slot = jnp.where(lane[:1] < n_p, row_slot, 1e6)
    earlier = (row_slot == slot) & (lane < place)
    before = (row_slot < slot) | earlier
    rank = jnp.sum(jnp.where(before, 1.0, 0.0), axis=1, keepdims=True)
    keep = jnp.where(jnp.sum(jnp.where(earlier, 1.0, 0.0), axis=1, keepdims=True) > 0, 1.0, 0.0)
    lane_f = lane.astype(F32)
    mine = rank == lane_f

    def ordered(values):
        return jnp.sum(jnp.where(mine, values, 0.0), axis=0, keepdims=True)

    last = jnp.sum(jnp.where(slot <= lane_f, 1.0, 0.0), axis=0, keepdims=True) - 1.0
    some = jnp.sum(jnp.where(slot == lane_f, 1.0, 0.0), axis=0, keepdims=True)
    last = jnp.where(some > 0, last, float(n_p))
    zero = jnp.zeros((1, width), F32)
    table = jnp.concatenate(
        [ordered(a_id), ordered(b_id), last, zero, zero, zero, zero, zero], axis=0
    ).astype(jnp.int32)
    which = iota(table.shape, 0)
    top = jnp.where(which == 0, n_a - 1, jnp.where(which == 1, n_g * kb - 1, n_p))
    tab_int[...] = jnp.clip(table, 0, top)
    tab_scale[...] = jnp.concatenate(
        [ordered(weight), ordered(keep), zero, zero, zero, zero, zero, zero], axis=0
    )


def kernel(
    dims, a_hbm, b_hbm, a_scale, a_rows, a_cols, b_scale, b_cols, c_rows, c_cols, out_hbm,
    a_own, a_pair, b_first, b_second, raw_own, raw_pair, meta, meta_x, meta_y, meta_z,
    tab_int1, tab_scale1, ids1, scales1, tab_int2, tab_scale2, ids2, scales2,
    acc, prod1, prod2, prod3, to_right, to_left, from_left, from_right, to_mirror, from_mirror, to_pair, from_pair,
    result,
    local_sem, meta_send, meta_recv, ring_send, ring_recv, core_send, core_recv, raw_send, raw_recv, a_send, a_recv,
    r_send, r_recv, l_send, l_recv, m_send, m_recv, p_send, p_recv, out_sem,
):
    n_x, n_y, n_r, a_cap, per, kb, c_cap = dims
    n_z = n_r // 2
    n_g = n_r * per
    n_c = n_y * a_cap
    half = b_first.shape[2]
    quarter = half // 2
    row, col, dep = lax.axis_index("row"), lax.axis_index("col"), lax.axis_index("depth")
    z, core = row // 2, row % 2

    def at_z(step):
        return (lax.rem(z + step + n_z, n_z) * 2 + core, col, dep)

    def at_y(step):
        return (row, lax.rem(col + step + n_y, n_y), dep)

    def at_x(step):
        return (row, col, lax.rem(dep + step + n_x, n_x))

    sibling = (z * 2 + 1 - core, col, dep)
    d_pair, d_mirror, d_far = dep + 1 - 2 * (dep % 2), n_x - 1 - dep, lax.rem(dep + 2, n_x)
    pair, mirror = (row, col, d_pair), (row, col, d_mirror)
    side = ((dep + 1) // 2) % 2
    first_cols, second_cols = pl.ds(0, half), pl.ds(half, half)
    low_lanes = iota((1, half), 1) < quarter

    meta[...] = jnp.zeros_like(meta)
    meta[0:1, 0:a_cap] = a_scale[...]
    meta[1:2, 0:a_cap] = a_rows[...].astype(F32)
    meta[2:3, 0:a_cap] = a_cols[...].astype(F32)
    meta[3 : 3 + per, 0:kb] = b_scale[...]
    meta[5 : 5 + per, 0:kb] = b_cols[...].astype(F32)
    meta[7:8, 0:c_cap] = c_rows[...].astype(F32) * ROW_KEY + c_cols[...].astype(F32)

    barrier = pltpu.get_barrier_semaphore()
    partners = [sibling, at_z(1), at_z(-1)] + [at_y(j) for j in range(1, n_y)] + [at_x(j) for j in range(1, n_x)]
    for partner in partners:
        pl.semaphore_signal(barrier, inc=1, device_id=partner, device_id_type=MESH)
    pl.semaphore_wait(barrier, len(partners))

    sends = []

    def copy(src, dst, send, recv, device):
        return pltpu.make_async_remote_copy(
            src_ref=src, dst_ref=dst, send_sem=send, recv_sem=recv, device_id=device, device_id_type=MESH
        )

    def push(src, dst, send, recv, device):
        made = copy(src, dst, send, recv, device)
        made.start()
        sends.append(made)

    def pulled(dst, send, recv):
        copy(dst, dst, send, recv, sibling).wait_recv()

    count = 0
    meta_waits = []
    for j in range(1, n_y):
        push(meta, meta_y.at[0, col], meta_send.at[count], meta_recv.at[count], at_y(j))
        meta_waits.append((meta_y.at[0, lax.rem(col - j + n_y, n_y)], count))
        count += 1
    for j in range(1, n_x):
        push(meta, meta_x.at[dep], meta_send.at[count], meta_recv.at[count], at_x(j))
        meta_waits.append((meta_x.at[lax.rem(dep - j + n_x, n_x)], count))
        count += 1
    push(meta, meta_z.at[0, row], meta_send.at[count], meta_recv.at[count], sibling)
    meta_waits.append((meta_z.at[0, z * 2 + 1 - core], count))
    count += 1
    hops_up, hops_down = n_z // 2, (n_z - 1) // 2
    ring_meta = count
    push(meta, meta_z.at[0, row], meta_send.at[count], meta_recv.at[count], at_z(1))
    push(meta, meta_z.at[0, row], meta_send.at[count + 1], meta_recv.at[count + 1], at_z(-1))
    count += 2 * hops_up
    core_meta = count
    count += 2 * hops_up
    pair_meta = count

    up, down = at_z(1), at_z(-1)
    units = [(kind, inner) for kind in range(2) for inner in range(per)]
    n_u = len(units)

    def b_unit(origin_z, origin_core, unit):
        kind, inner = units[unit]
        refs = b_second if kind else b_first
        return refs.at[pl.ds(((origin_z * 2 + origin_core) * per + inner) * kb, kb)]

    def a_part(kind, origin, first):
        refs = a_pair if kind else a_own
        return refs.at[pl.ds(origin * a_cap + first, a_cap // 2)]

    def ring_slot(direction, step, unit):
        return (direction * hops_up + step) * n_u + unit

    def hops(direction, unit):
        return hops_up if units[unit][1] == direction else hops_down

    def send_first(src, unit):
        for direction, device in ((0, up), (1, down)):
            index = ring_slot(direction, 0, unit)
            push(src, b_unit(z, core, unit), ring_send.at[index], ring_recv.at[index], device)
        push(src, b_unit(z, core, unit), core_send.at[unit], core_recv.at[unit], sibling)

    for inner in range(per):
        send_first(b_hbm.at[inner, :, :, first_cols], inner)
    for inner in range(per):
        push(b_hbm.at[inner, :, :, second_cols], raw_pair.at[inner], raw_send.at[inner], raw_recv.at[inner], pair)

    mid = a_cap // 2
    y_up, y_down = at_y(1), at_y(-1)
    left, right, across = at_y(-1)[1], at_y(1)[1], at_y(2)[1]

    def own_a(first, slot, device):
        push(a_hbm.at[pl.ds(first, mid)], a_part(0, col, first), a_send.at[slot], a_recv.at[slot], device)

    own_a(0, 0, y_up)
    own_a(mid, 3, y_down)
    own_a(mid, 1, y_up)
    own_a(0, 4, y_down)
    for number in range(2):
        first, slot = number * mid, 12 + number
        push(a_hbm.at[pl.ds(first, mid)], a_part(1, col, first), a_send.at[slot], a_recv.at[slot], pair)
    local = [
        pltpu.make_async_copy(a_hbm, a_own.at[pl.ds(col * a_cap, a_cap)], local_sem.at[0]),
    ]
    for inner in range(per):
        local.append(
            pltpu.make_async_copy(b_hbm.at[inner, :, :, first_cols], b_unit(z, core, inner), local_sem.at[1 + inner])
        )
    local_raw = [
        pltpu.make_async_copy(b_hbm.at[inner, :, :, second_cols], raw_own.at[inner], local_sem.at[3 + inner])
        for inner in range(per)
    ]
    for made in local + local_raw:
        made.start()
    meta_x[dep] = meta[...]
    meta_y[0, col] = meta[...]
    meta_z[0, row] = meta[...]

    def forward_meta(step):
        for direction, limit in ((0, hops_up), (1, hops_down)):
            if step >= limit:
                continue
            origin_z = lax.rem(z - step - 1 + n_z, n_z) if direction == 0 else lax.rem(z + step + 1, n_z)
            here = meta_z.at[0, origin_z * 2 + core]
            index = ring_meta + 2 * step + direction
            pulled(here, meta_send.at[index], meta_recv.at[index])
            if step + 1 < limit:
                push(here, here, meta_send.at[index + 2], meta_recv.at[index + 2], up if direction == 0 else down)
            index = core_meta + 2 * step + direction
            push(here, here, meta_send.at[index], meta_recv.at[index], sibling)
            meta_waits.append((meta_z.at[0, origin_z * 2 + 1 - core], index))

    def pair_tables():
        for here, index in meta_waits:
            pulled(here, meta_send.at[index], meta_recv.at[index])
        push(meta_y.at[0], meta_y.at[1], meta_send.at[pair_meta], meta_recv.at[pair_meta], pair)
        push(meta_z.at[0], meta_z.at[1], meta_send.at[pair_meta + 1], meta_recv.at[pair_meta + 1], pair)

    core_waits = [[(b_unit(z, 1 - core, kind * per + inner), kind * per + inner) for inner in range(per)] for kind in range(2)]

    def pack(inner):
        pulled(raw_pair.at[inner], raw_send.at[inner], raw_recv.at[inner])
        base = (row * per + inner) * kb
        for t in range(kb):
            mine, other = raw_own[inner, t].astype(F32), raw_pair[inner, t].astype(F32)
            mine = jnp.where(side == 0, mine, pltpu.roll(mine, quarter, 1))
            other = jnp.where(side == 0, pltpu.roll(other, quarter, 1), other)
            b_second[base + t] = jnp.where(low_lanes, mine, other).astype(b_second.dtype)

    def forward_b(step, unit):
        for direction in range(2):
            limit = hops(direction, unit)
            if step >= limit:
                continue
            origin_z = lax.rem(z - step - 1 + n_z, n_z) if direction == 0 else lax.rem(z + step + 1, n_z)
            here = b_unit(origin_z, core, unit)
            index = ring_slot(direction, step, unit)
            pulled(here, ring_send.at[index], ring_recv.at[index])
            if step + 1 < limit:
                index = ring_slot(direction, step + 1, unit)
                push(here, here, ring_send.at[index], ring_recv.at[index], up if direction == 0 else down)
            index = n_u + ring_slot(direction, step, unit)
            push(here, here, core_send.at[index], core_recv.at[index], sibling)
            core_waits[units[unit][0]].append((b_unit(origin_z, 1 - core, unit), index))

    def arrived(kind, origin, first, slot):
        here = a_part(kind, origin, first)
        pulled(here, a_send.at[slot], a_recv.at[slot])
        return here

    def hand_on(here, slot, device):
        push(here, here, a_send.at[slot], a_recv.at[slot], device)

    def finish(kind):
        for here, index in core_waits[kind]:
            pulled(here, core_send.at[index], core_recv.at[index])

    def plan(kind, tab_int, tab_scale, ids, scales, sem):
        schedule(dims, kind, meta_x, meta_y, meta_z, tab_int, tab_scale)
        made = [
            pltpu.make_async_copy(tab_int, ids, local_sem.at[sem]),
            pltpu.make_async_copy(tab_scale, scales, local_sem.at[sem + 1]),
        ]
        for one in made:
            one.start()
        return made

    def bounded(index, size):
        return jnp.clip(index, 0, size - 1)

    def multiply(a_refs, b_refs, ids, scales, prod):
        n_p = kb * n_c
        acc[...] = jnp.zeros_like(acc)
        prod[n_p] = jnp.zeros(prod.shape[1:], prod.dtype)

        @pl.loop(0, n_p, unroll=16)
        def _(j):
            left_block = a_refs[bounded(ids[0, j], n_c)]
            right_block = b_refs[bounded(ids[1, j], n_g * kb)]
            product = jnp.dot(left_block, right_block, preferred_element_type=F32)
            total = acc[...] * scales[1, j] + product * scales[0, j]
            acc[...] = total
            prod[j] = total.astype(prod.dtype)

    piece = 2
    half_c = c_cap // 2
    steps = half_c // piece
    x_up, x_down = at_x(1), at_x(-1)
    d_right, d_left = x_up[2], x_down[2]
    dtype = result.dtype

    def own1(dest, index):
        return prod1[bounded(ids1[2, dest * c_cap + index], prod1.shape[0])]

    def part(refs, stage, k):
        return refs.at[pl.ds(stage * half_c + k * piece, piece)]

    def send_right(stage, k):
        index = stage * steps + k
        return copy(part(to_right, stage, k), part(from_left, stage, k), r_send.at[index], r_recv.at[index], x_up)

    def send_left(stage, k):
        index = stage * steps + k
        return copy(part(to_left, stage, k), part(from_right, stage, k), l_send.at[index], l_recv.at[index], x_down)

    def wait_left(stage, k):
        here, index = part(from_left, stage, k), stage * steps + k
        copy(here, here, r_send.at[index], r_recv.at[index], x_up).wait_recv()

    def wait_right(stage, k):
        here, index = part(from_right, stage, k), stage * steps + k
        copy(here, here, l_send.at[index], l_recv.at[index], x_down).wait_recv()

    def first_sends():
        @pl.loop(0, steps)
        def _(k):
            for i in range(piece):
                to_right[k * piece + i] = own1(d_far, k * piece + i)
            send_right(0, k).start()
            for i in range(piece):
                to_left[k * piece + i] = own1(d_far, half_c + k * piece + i)
            send_left(0, k).start()

        @pl.loop(0, steps)
        def _(k):
            for i in range(piece):
                to_right[half_c + k * piece + i] = own1(d_right, half_c + k * piece + i)
            send_right(1, k).start()
            for i in range(piece):
                to_left[half_c + k * piece + i] = own1(d_left, k * piece + i)
            send_left(1, k).start()

    def pass_sums(first, last):
        @pl.loop(first, last)
        def _(k):
            wait_left(0, k)
            for i in range(piece):
                m = k * piece + i
                total = own1(d_right, m).astype(F32) + from_left[m].astype(F32)
                to_right[2 * half_c + m] = total.astype(dtype)
            send_right(2, k).start()
            wait_right(0, k)
            for i in range(piece):
                m = k * piece + i
                total = own1(d_left, half_c + m).astype(F32) + from_right[m].astype(F32)
                to_left[2 * half_c + m] = total.astype(dtype)
            send_left(2, k).start()

    def first_results():
        @pl.loop(0, steps)
        def _(k):
            wait_right(1, k)
            wait_left(2, k)
            for i in range(piece):
                m = k * piece + i
                total = own1(dep, m).astype(F32) + from_left[2 * half_c + m].astype(F32)
                result[m, :, 0:half] = (total + from_right[half_c + m].astype(F32)).astype(dtype)
            wait_left(1, k)
            wait_right(2, k)
            for i in range(piece):
                m = k * piece + i
                total = own1(dep, half_c + m).astype(F32) + from_right[2 * half_c + m].astype(F32)
                result[half_c + m, :, 0:half] = (total + from_left[half_c + m].astype(F32)).astype(dtype)

    def packed(dest, u):
        def take(prod, ids, index):
            return prod[bounded(ids[2, dest * c_cap + index], prod.shape[0])].astype(F32)

        mine = take(prod2, ids1, u), take(prod2, ids1, half_c + u)
        other = take(prod3, ids2, u), take(prod3, ids2, half_c + u)
        straight, crossed = jnp.where(low_lanes, mine[0], other[1]), jnp.where(low_lanes, mine[1], other[0])
        return straight + pltpu.roll(crossed, quarter, 1)

    def send_mirror(stage, k):
        index = stage * steps + k
        return copy(part(to_mirror, stage, k), part(from_mirror, stage, k), m_send.at[index], m_recv.at[index], mirror)

    def send_pair(k):
        return copy(part(to_pair, 0, k), part(from_pair, 0, k), p_send.at[k], p_recv.at[k], pair)

    def write(number, k):
        here = pl.ds(number * half_c + k * piece, piece)
        return pltpu.make_async_copy(result.at[here], out_hbm.at[here], out_sem.at[number * steps + k])

    def second_sends():
        for stage, dest in ((0, d_far), (1, d_mirror)):

            @pl.loop(0, steps)
            def _(k):
                for i in range(piece):
                    u = k * piece + i
                    to_mirror[stage * half_c + u] = packed(dest, u).astype(dtype)
                send_mirror(stage, k).start()

    def second_results():
        @pl.loop(0, steps)
        def _(k):
            send_mirror(0, k).wait_recv()
            for i in range(piece):
                u = k * piece + i
                to_pair[u] = (packed(d_pair, u) + from_mirror[u].astype(F32)).astype(dtype)
            send_pair(k).start()

        @pl.loop(0, steps)
        def _(k):
            send_pair(k).wait_recv()
            send_mirror(1, k).wait_recv()
            for i in range(piece):
                u = k * piece + i
                mine = packed(dep, u) + from_mirror[half_c + u].astype(F32)
                other = from_pair[u].astype(F32)
                low = jnp.where(side == 0, mine, other)
                high = jnp.where(side == 0, other, mine)
                result[u, :, half : 2 * half] = jnp.where(low_lanes, low, pltpu.roll(high, quarter, 1)).astype(dtype)
                result[half_c + u, :, half : 2 * half] = jnp.where(
                    low_lanes, pltpu.roll(low, quarter, 1), high
                ).astype(dtype)
            write(0, k).start()
            write(1, k).start()

    forward_meta(0)
    forward_b(0, 0)
    for made in local_raw:
        made.wait()
    forward_b(0, 1)
    forward_meta(1)
    for inner in range(per):
        pack(inner)
    hand_on(arrived(0, left, 0, 0), 2, y_up)
    hand_on(arrived(0, right, mid, 3), 5, y_down)
    forward_b(1, 0)
    forward_meta(2)
    forward_b(1, 1)
    forward_meta(3)
    forward_b(2, 0)
    own_packed = [b_unit(z, core, per + inner) for inner in range(per)]
    send_first(own_packed[0], per)
    pair_tables()
    table1 = plan(0, tab_int1, tab_scale1, ids1, scales1, 5)
    forward_b(2, 1)
    send_first(own_packed[1], per + 1)
    arrived(0, left, mid, 1)
    arrived(0, right, 0, 4)
    low_a, high_a = arrived(1, col, 0, 12), arrived(1, col, mid, 13)
    hand_on(low_a, 6, y_up)
    hand_on(high_a, 9, y_down)
    hand_on(high_a, 7, y_up)
    hand_on(low_a, 10, y_down)
    forward_b(3, 0)
    forward_b(3, 1)
    arrived(0, across, 0, 2)
    arrived(0, across, mid, 5)
    for made in table1 + local:
        made.wait()
    finish(0)
    forward_b(0, 2)
    multiply(a_own, b_first, ids1, scales1, prod1)
    first_sends()
    forward_b(0, 3)
    hand_on(arrived(1, left, 0, 6), 8, y_up)
    hand_on(arrived(1, right, mid, 9), 11, y_down)
    forward_b(1, 2)
    pulled(meta_y.at[1], meta_send.at[pair_meta], meta_recv.at[pair_meta])
    pulled(meta_z.at[1], meta_send.at[pair_meta + 1], meta_recv.at[pair_meta + 1])
    table2 = plan(1, tab_int2, tab_scale2, ids2, scales2, 7)
    forward_b(1, 3)
    pass_sums(0, 2)
    forward_b(2, 2)
    pass_sums(2, 4)
    forward_b(2, 3)
    pass_sums(4, steps)
    forward_b(3, 2)
    forward_b(3, 3)
    finish(1)
    multiply(a_own, b_second, ids1, scales1, prod2)
    arrived(1, left, mid, 7)
    arrived(1, right, 0, 10)
    arrived(1, across, 0, 8)
    arrived(1, across, mid, 11)
    for made in table2:
        made.wait()
    multiply(a_pair, b_second, ids2, scales2, prod3)
    second_sends()
    first_results()
    second_results()

    @pl.loop(0, steps)
    def _(k):
        write(0, k).wait()
        write(1, k).wait()
        send_pair(k).wait_send()
        for stage in range(2):
            send_mirror(stage, k).wait_send()
        for stage in range(3):
            send_right(stage, k).wait_send()
            send_left(stage, k).wait_send()

    for made in sends:
        made.wait_send()


def shards(a_blocks, a_scale, a_rows, a_cols, b_blocks, b_scale, b_cols, c_rows, c_cols):
    edge = a_blocks.shape[1]
    half = edge // 2
    a_cap, c_cap = a_blocks.shape[0], c_rows.shape[0]
    per, kb = b_blocks.shape[0], b_blocks.shape[3]
    n_r, n_y, n_x = lax.axis_size("row"), lax.axis_size("col"), lax.axis_size("depth")
    dims = (n_x, n_y, n_r, a_cap, per, kb, c_cap)
    n_c = n_y * a_cap
    half_c = c_cap // 2

    width = -(-kb * n_c // LANES) * LANES

    dtype = a_blocks.dtype
    block, part = (edge, edge), (edge, half)
    dma = pltpu.SemaphoreType.DMA
    hops = n_r // 4
    n_meta = (n_y - 1) + (n_x - 1) + 1 + 4 * hops + 2
    n_ring = 2 * hops * 2 * per
    any_space = pl.BlockSpec(memory_space=pl.ANY)
    vmem = pl.BlockSpec(memory_space=pltpu.VMEM)
    return pl.pallas_call(
        functools.partial(kernel, dims),
        out_shape=jax.ShapeDtypeStruct((c_cap,) + block, dtype),
        in_specs=[any_space, any_space] + [vmem] * 7,
        out_specs=any_space,
        scratch_shapes=[
            pltpu.VMEM((n_c,) + block, dtype),
            pltpu.VMEM((n_c,) + block, dtype),
            pltpu.VMEM((n_r * per * kb,) + part, dtype),
            pltpu.VMEM((n_r * per * kb,) + part, dtype),
            pltpu.VMEM((per, kb) + part, dtype),
            pltpu.VMEM((per, kb) + part, dtype),
            pltpu.VMEM((8, LANES), F32),
            pltpu.VMEM((n_x, 8, LANES), F32),
            pltpu.VMEM((2, n_y, 8, LANES), F32),
            pltpu.VMEM((2, n_r, 8, LANES), F32),
        ]
        + [
            space((8, width), kind)
            for _ in range(2)
            for space in (pltpu.VMEM, pltpu.SMEM)
            for kind in (jnp.int32, F32)
        ]
        + [
            pltpu.VMEM(part, F32),
        ]
        + [pltpu.VMEM((kb * n_c + 1,) + part, dtype)] * 3
        + [pltpu.VMEM((3 * half_c,) + part, dtype)] * 4
        + [pltpu.VMEM((2 * half_c,) + part, dtype)] * 2
        + [pltpu.VMEM((half_c,) + part, dtype)] * 2
        + [
            pltpu.VMEM((c_cap,) + block, dtype),
            dma((9,)),
            dma((n_meta,)),
            dma((n_meta,)),
            dma((n_ring,)),
            dma((n_ring,)),
            dma((2 * per + n_ring,)),
            dma((2 * per + n_ring,)),
            dma((per,)),
            dma((per,)),
            dma((14,)),
            dma((14,)),
        ]
        + [dma((3 * half_c,))] * 4
        + [dma((2 * half_c,))] * 2
        + [dma((half_c,))] * 2
        + [dma((c_cap,))],
        compiler_params=pltpu.CompilerParams(
            collective_id=0, has_side_effects=True, vmem_limit_bytes=62 * 1024 * 1024
        ),
    )(
        a_blocks,
        b_blocks.reshape(per, kb, edge, edge),
        a_scale.reshape(1, a_cap),
        a_rows.reshape(1, a_cap),
        a_cols.reshape(1, a_cap),
        b_scale.reshape(per, kb),
        b_cols.reshape(per, kb),
        c_rows.reshape(1, c_cap),
        c_cols.reshape(1, c_cap),
    )


def solution(mesh):
    return jax.shard_map(
        shards,
        mesh=mesh,
        in_specs=(
            P(("row", "col", "depth"), None, None),
            P(("row", "col", "depth")),
            P(("row", "col", "depth")),
            P(("row", "col", "depth")),
            P("row", "col", "depth", None, None, None),
            P("row", "col", "depth", None),
            P("row", "col", "depth", None),
            P(("row", "col", "depth")),
            P(("row", "col", "depth")),
        ),
        out_specs=P(("row", "col", "depth"), None, None),
        check_vma=False,
    )
```

```python
import functools

import jax
import jax.numpy as jnp
from jax import lax
from jax.experimental import pallas as pl
from jax.experimental.pallas import tpu as pltpu
from jax.sharding import PartitionSpec as P

MESH = pl.DeviceIdType.MESH
LANES = 128
ROW_KEY = 1024.0
F32 = jnp.float32


def iota(shape, dim):
    return lax.broadcasted_iota(jnp.int32, shape, dim)


def schedule(dims, kind, meta_x, meta_y, meta_z, tab_int, tab_scale):
    n_x, n_y, n_r, a_cap, per, kb, c_cap = dims
    n_a = n_y * a_cap
    n_g = n_r * per
    n_slots = n_x * c_cap
    eye = iota((a_cap, LANES), 0) == iota((a_cap, LANES), 1)
    lane = iota((n_a, LANES), 1)

    def column(which):
        parts = [
            jnp.sum(jnp.where(eye, meta_y[kind, c, which : which + 1, :], 0.0), axis=1, keepdims=True)
            for c in range(n_y)
        ]
        return jnp.concatenate(parts, axis=0)

    a_scale, a_rows, a_cols = column(0), column(1), column(2)
    group = a_cols.astype(jnp.int32) // n_x
    b_scale = jnp.zeros((n_a, LANES), F32)
    b_cols = jnp.zeros((n_a, LANES), F32)
    for g in range(n_g):
        here = group == g
        d, i = g // per, g % per
        b_scale = jnp.where(here, meta_z[kind, d, 3 + i : 4 + i, :], b_scale)
        b_cols = jnp.where(here, meta_z[kind, d, 5 + i : 6 + i, :], b_cols)
    device, inner = group // per, group % per
    slots, weights, b_ids, first_ids = [], [], [], []
    for t in range(kb):
        col = jnp.sum(jnp.where(lane == t, b_cols, 0.0), axis=1, keepdims=True)
        scale = jnp.sum(jnp.where(lane == t, b_scale, 0.0), axis=1, keepdims=True)
        key = a_rows * ROW_KEY + col
        found = jnp.zeros((n_a, LANES), F32)
        for e in range(n_x):
            hit = (key == meta_x[e, 7:8, :]) & (lane < c_cap)
            found = jnp.where(hit, (lane + (e * c_cap + 1)).astype(F32), found)
        slot = jnp.max(found, axis=1, keepdims=True)
        slots.append(jnp.where(slot > 0, slot - 1, float(n_slots)))
        weights.append(a_scale * scale)
        b_ids.append((group * kb + t).astype(F32))
        first_ids.append((device * kb + t).astype(F32))
    slot, weight = jnp.concatenate(slots, axis=0), jnp.concatenate(weights, axis=0)
    a_id = jnp.concatenate([iota((n_a, 1), 0).astype(F32)] * kb, axis=0)
    b_id, first_id = jnp.concatenate(b_ids, axis=0), jnp.concatenate(first_ids, axis=0)
    low = jnp.where(jnp.concatenate([inner] * kb, axis=0) == 0, weight, 0.0)
    n_p = kb * n_a
    width = tab_int.shape[1]
    place, lane = iota((n_p, width), 0), iota((n_p, width), 1)
    row_slot = jnp.sum(jnp.where(place == lane, slot, 0.0), axis=0, keepdims=True)
    row_slot = jnp.where(lane[:1] < n_p, row_slot, 1e6)
    earlier = (row_slot == slot) & (lane < place)
    before = (row_slot < slot) | earlier
    rank = jnp.sum(jnp.where(before, 1.0, 0.0), axis=1, keepdims=True)
    keep = jnp.where(jnp.sum(jnp.where(earlier, 1.0, 0.0), axis=1, keepdims=True) > 0, 1.0, 0.0)
    lane_f = lane.astype(F32)
    mine = rank == lane_f

    def ordered(values):
        return jnp.sum(jnp.where(mine, values, 0.0), axis=0, keepdims=True)

    last = jnp.sum(jnp.where(slot <= lane_f, 1.0, 0.0), axis=0, keepdims=True) - 1.0
    some = jnp.sum(jnp.where(slot == lane_f, 1.0, 0.0), axis=0, keepdims=True)
    last = jnp.where(some > 0, last, float(n_p))
    zero = jnp.zeros((1, width), F32)
    table = jnp.concatenate(
        [ordered(a_id), ordered(b_id), last, ordered(first_id), zero, zero, zero, zero], axis=0
    ).astype(jnp.int32)
    which = iota(table.shape, 0)
    top = jnp.where(which == 0, n_a - 1, jnp.where(which == 1, n_g * kb - 1, n_p))
    top = jnp.where(which == 3, n_r * kb - 1, top)
    tab_int[...] = jnp.clip(table, 0, top)
    tab_scale[...] = jnp.concatenate(
        [ordered(weight), ordered(keep), ordered(low), ordered(weight - low), zero, zero, zero, zero], axis=0
    )


def kernel(
    dims, a_hbm, b_hbm, a_scale, a_rows, a_cols, b_scale, b_cols, c_rows, c_cols, out_hbm,
    a_own0, a_own1, a_pair0, a_pair1, b_one, b_two, b_second, raw_own, raw_pair, meta, meta_x, meta_y, meta_z,
    tab_int1, tab_scale1, ids1, scales1, tab_int2, tab_scale2, ids2, scales2,
    acc, prod0, prod1, prod2, prod3, prod4, prod5, prod6, prod7,
    to_right, to_left, from_left, from_right, to_mirror, from_mirror, to_pair, from_pair, result,
    local_sem, meta_send, meta_recv, ring_send, ring_recv, core_send, core_recv, raw_send, raw_recv, a_send, a_recv,
    r_send, r_recv, l_send, l_recv, m_send, m_recv, p_send, p_recv, out_sem,
):
    n_x, n_y, n_r, a_cap, per, kb, c_cap = dims
    n_z = n_r // 2
    n_g = n_r * per
    n_c = n_y * a_cap
    half = b_second.shape[2]
    quarter = half // 2
    a_own, a_pair = (a_own0, a_own1), (a_pair0, a_pair1)
    first_prod = ((prod0, prod1), (prod2, prod3))
    own_prod, pair_prod = (prod4, prod5), (prod6, prod7)
    row, col, dep = lax.axis_index("row"), lax.axis_index("col"), lax.axis_index("depth")
    z, core = row // 2, row % 2

    def at_z(step):
        return (lax.rem(z + step + n_z, n_z) * 2 + core, col, dep)

    def at_y(step):
        return (row, lax.rem(col + step + n_y, n_y), dep)

    def at_x(step):
        return (row, col, lax.rem(dep + step + n_x, n_x))

    sibling = (z * 2 + 1 - core, col, dep)
    d_pair, d_mirror, d_far = dep + 1 - 2 * (dep % 2), n_x - 1 - dep, lax.rem(dep + 2, n_x)
    pair, mirror = (row, col, d_pair), (row, col, d_mirror)
    side = ((dep + 1) // 2) % 2
    second_cols = pl.ds(half, half)
    low_lanes = iota((1, half), 1) < quarter

    meta[...] = jnp.zeros_like(meta)
    meta[0:1, 0:a_cap] = a_scale[...]
    meta[1:2, 0:a_cap] = a_rows[...].astype(F32)
    meta[2:3, 0:a_cap] = a_cols[...].astype(F32)
    meta[3 : 3 + per, 0:kb] = b_scale[...]
    meta[5 : 5 + per, 0:kb] = b_cols[...].astype(F32)
    meta[7:8, 0:c_cap] = c_rows[...].astype(F32) * ROW_KEY + c_cols[...].astype(F32)

    barrier = pltpu.get_barrier_semaphore()
    partners = [sibling, at_z(1), at_z(-1)] + [at_y(j) for j in range(1, n_y)] + [at_x(j) for j in range(1, n_x)]
    for partner in partners:
        pl.semaphore_signal(barrier, inc=1, device_id=partner, device_id_type=MESH)
    local_raw = pltpu.make_async_copy(b_hbm, raw_own, local_sem.at[0])
    local_raw.start()
    local_raw.wait()
    for t in range(kb):
        one, two = raw_own[0, t, :, 0:half].astype(F32), raw_own[1, t, :, 0:half].astype(F32)
        b_one[row * kb + t] = jnp.where(low_lanes, one, pltpu.roll(two, quarter, 1)).astype(b_one.dtype)
        b_two[row * kb + t] = jnp.where(low_lanes, pltpu.roll(one, quarter, 1), two).astype(b_two.dtype)
    pl.semaphore_wait(barrier, len(partners))

    sends = []

    def copy(src, dst, send, recv, device):
        return pltpu.make_async_remote_copy(
            src_ref=src, dst_ref=dst, send_sem=send, recv_sem=recv, device_id=device, device_id_type=MESH
        )

    def push(src, dst, send, recv, device):
        made = copy(src, dst, send, recv, device)
        made.start()
        sends.append(made)

    def pulled(dst, send, recv):
        copy(dst, dst, send, recv, sibling).wait_recv()

    count = 0
    meta_waits = []
    for j in range(1, n_y):
        push(meta, meta_y.at[0, col], meta_send.at[count], meta_recv.at[count], at_y(j))
        meta_waits.append((meta_y.at[0, lax.rem(col - j + n_y, n_y)], count))
        count += 1
    for j in range(1, n_x):
        push(meta, meta_x.at[dep], meta_send.at[count], meta_recv.at[count], at_x(j))
        meta_waits.append((meta_x.at[lax.rem(dep - j + n_x, n_x)], count))
        count += 1
    push(meta, meta_z.at[0, row], meta_send.at[count], meta_recv.at[count], sibling)
    meta_waits.append((meta_z.at[0, z * 2 + 1 - core], count))
    count += 1
    hops_up, hops_down = n_z // 2, (n_z - 1) // 2
    ring_meta = count
    push(meta, meta_z.at[0, row], meta_send.at[count], meta_recv.at[count], at_z(1))
    push(meta, meta_z.at[0, row], meta_send.at[count + 1], meta_recv.at[count + 1], at_z(-1))
    count += 2 * hops_up
    core_meta = count
    count += 2 * hops_up
    pair_meta = count

    up, down = at_z(1), at_z(-1)
    units = [(b_one, kb, t, 1, t // 2) for t in range(kb)]
    units += [(b_two, kb, t, 1, 1 - t // 2) for t in range(kb)]
    units += [(b_second, per * kb, inner * kb, kb, inner) for inner in range(per)]
    n_u = len(units)
    unit_one, unit_two = list(range(kb)), list(range(kb, 2 * kb))
    unit_second = list(range(2 * kb, 2 * kb + per))

    def b_unit(origin_z, origin_core, unit):
        refs, each, first, size, _ = units[unit]
        return refs.at[pl.ds((origin_z * 2 + origin_core) * each + first, size)]

    def a_part(refs, origin, first):
        return refs.at[pl.ds(origin * a_cap + first, a_cap // 2)]

    def ring_slot(direction, step, unit):
        return (direction * hops_up + step) * n_u + unit

    def hops(direction, unit):
        return hops_up if units[unit][4] == direction else hops_down

    def send_first(src, unit):
        for direction, device in ((0, up), (1, down)):
            index = ring_slot(direction, 0, unit)
            push(src, b_unit(z, core, unit), ring_send.at[index], ring_recv.at[index], device)
        push(src, b_unit(z, core, unit), core_send.at[unit], core_recv.at[unit], sibling)

    for unit in unit_one:
        send_first(b_unit(z, core, unit), unit)
    for inner in range(per):
        push(raw_own.at[inner, :, :, second_cols], raw_pair.at[inner], raw_send.at[inner], raw_recv.at[inner], pair)

    mid = a_cap // 2
    y_up, y_down = at_y(1), at_y(-1)
    left, right, across = at_y(-1)[1], at_y(1)[1], at_y(2)[1]

    def a_rows_of(rr, first):
        return a_hbm.at[pl.ds(first, mid), pl.ds(rr * half, half)]

    def send_own_a(rr):
        for first, slot, device in ((0, 0, y_up), (mid, 3, y_down), (mid, 1, y_up), (0, 4, y_down)):
            index = rr * 14 + slot
            push(a_rows_of(rr, first), a_part(a_own[rr], col, first), a_send.at[index], a_recv.at[index], device)

    def send_raw_a(rr):
        for number in range(2):
            first, index = number * mid, rr * 14 + 12 + number
            push(a_rows_of(rr, first), a_part(a_pair[rr], col, first), a_send.at[index], a_recv.at[index], pair)

    send_own_a(0)
    send_raw_a(0)
    local = [
        pltpu.make_async_copy(
            a_hbm.at[:, pl.ds(rr * half, half)], a_own[rr].at[pl.ds(col * a_cap, a_cap)], local_sem.at[1 + rr]
        )
        for rr in range(2)
    ]
    for made in local:
        made.start()
    meta_x[dep] = meta[...]
    meta_y[0, col] = meta[...]
    meta_z[0, row] = meta[...]

    def forward_meta(step):
        for direction, limit in ((0, hops_up), (1, hops_down)):
            if step >= limit:
                continue
            origin_z = lax.rem(z - step - 1 + n_z, n_z) if direction == 0 else lax.rem(z + step + 1, n_z)
            here = meta_z.at[0, origin_z * 2 + core]
            index = ring_meta + 2 * step + direction
            pulled(here, meta_send.at[index], meta_recv.at[index])
            if step + 1 < limit:
                push(here, here, meta_send.at[index + 2], meta_recv.at[index + 2], up if direction == 0 else down)
            index = core_meta + 2 * step + direction
            push(here, here, meta_send.at[index], meta_recv.at[index], sibling)
            meta_waits.append((meta_z.at[0, origin_z * 2 + 1 - core], index))

    def pair_tables():
        for here, index in meta_waits:
            pulled(here, meta_send.at[index], meta_recv.at[index])
        push(meta_y.at[0], meta_y.at[1], meta_send.at[pair_meta], meta_recv.at[pair_meta], pair)
        push(meta_z.at[0], meta_z.at[1], meta_send.at[pair_meta + 1], meta_recv.at[pair_meta + 1], pair)

    core_waits = [[(b_unit(z, 1 - core, unit), unit)] for unit in range(n_u)]

    def pack(inner):
        pulled(raw_pair.at[inner], raw_send.at[inner], raw_recv.at[inner])
        base = (row * per + inner) * kb
        for t in range(kb):
            mine, other = raw_own[inner, t, :, half : 2 * half].astype(F32), raw_pair[inner, t].astype(F32)
            mine = jnp.where(side == 0, mine, pltpu.roll(mine, quarter, 1))
            other = jnp.where(side == 0, pltpu.roll(other, quarter, 1), other)
            b_second[base + t] = jnp.where(low_lanes, mine, other).astype(b_second.dtype)

    def forward_b(step, unit):
        for direction in range(2):
            limit = hops(direction, unit)
            if step >= limit:
                continue
            origin_z = lax.rem(z - step - 1 + n_z, n_z) if direction == 0 else lax.rem(z + step + 1, n_z)
            here = b_unit(origin_z, core, unit)
            index = ring_slot(direction, step, unit)
            pulled(here, ring_send.at[index], ring_recv.at[index])
            if step + 1 < limit:
                index = ring_slot(direction, step + 1, unit)
                push(here, here, ring_send.at[index], ring_recv.at[index], up if direction == 0 else down)
            index = n_u + ring_slot(direction, step, unit)
            push(here, here, core_send.at[index], core_recv.at[index], sibling)
            core_waits[unit].append((b_unit(origin_z, 1 - core, unit), index))

    def arrived(refs, rr, origin, first, slot):
        here, index = a_part(refs[rr], origin, first), rr * 14 + slot
        pulled(here, a_send.at[index], a_recv.at[index])
        return here

    def hand_on(here, rr, slot, device):
        index = rr * 14 + slot
        push(here, here, a_send.at[index], a_recv.at[index], device)

    def across_a(refs, rr, base):
        hand_on(arrived(refs, rr, left, 0, base), rr, base + 2, y_up)
        hand_on(arrived(refs, rr, right, mid, base + 3), rr, base + 5, y_down)

    def rest_a(refs, rr, base):
        arrived(refs, rr, left, mid, base + 1)
        arrived(refs, rr, right, 0, base + 4)
        arrived(refs, rr, across, 0, base + 2)
        arrived(refs, rr, across, mid, base + 5)

    def spread_pair_a(rr):
        low_a, high_a = arrived(a_pair, rr, col, 0, 12), arrived(a_pair, rr, col, mid, 13)
        hand_on(low_a, rr, 6, y_up)
        hand_on(high_a, rr, 9, y_down)
        hand_on(high_a, rr, 7, y_up)
        hand_on(low_a, rr, 10, y_down)

    def finish(unit):
        for here, index in core_waits[unit]:
            pulled(here, core_send.at[index], core_recv.at[index])

    def plan(kind, tab_int, tab_scale, ids, scales, sem):
        schedule(dims, kind, meta_x, meta_y, meta_z, tab_int, tab_scale)
        made = [
            pltpu.make_async_copy(tab_int, ids, local_sem.at[sem]),
            pltpu.make_async_copy(tab_scale, scales, local_sem.at[sem + 1]),
        ]
        for one in made:
            one.start()
        return made

    def bounded(index, size):
        return jnp.clip(index, 0, size - 1)

    def multiply(a_refs, b_refs, ids, scales, prod, split):
        n_p = kb * n_c
        acc[...] = jnp.zeros_like(acc)
        prod[n_p] = jnp.zeros(prod.shape[1:], prod.dtype)

        @pl.loop(0, n_p, unroll=16)
        def _(j):
            left_block = a_refs[bounded(ids[0, j], n_c)]
            right_block = b_refs[bounded(ids[3 if split else 1, j], b_refs.shape[0])]
            product = jnp.dot(left_block, right_block, preferred_element_type=F32)
            weight = jnp.where(low_lanes, scales[2, j], scales[3, j]) if split else scales[0, j]
            total = acc[...] * scales[1, j] + product * weight
            acc[...] = total
            prod[j] = total.astype(prod.dtype)

    def folded(mine, other, dest, u, v):
        def take(which, index):
            prod, ids = which
            return prod[bounded(ids[2, dest * c_cap + index], prod.shape[0])].astype(F32)

        straight = jnp.where(low_lanes, take(mine, u), take(other, v))
        crossed = jnp.where(low_lanes, take(mine, v), take(other, u))
        return straight + pltpu.roll(crossed, quarter, 1)

    half_c = c_cap // 2
    pairs = half_c // 2
    x_up, x_down = at_x(1), at_x(-1)
    d_right, d_left = x_up[2], x_down[2]
    dtype = result.dtype

    def first_block(tile, dest, base, i):
        both = (first_prod[tile // 2][tile % 2], ids1)
        return folded(both, both, dest, base + i, base + pairs + i)

    def part(refs, tile, stage):
        return refs.at[pl.ds((tile * 3 + stage) * pairs, pairs)]

    def send_right(tile, stage):
        index = tile * 3 + stage
        return copy(part(to_right, tile, stage), part(from_left, tile, stage), r_send.at[index], r_recv.at[index], x_up)

    def send_left(tile, stage):
        index = tile * 3 + stage
        return copy(part(to_left, tile, stage), part(from_right, tile, stage), l_send.at[index], l_recv.at[index], x_down)

    def wait_left(tile, stage):
        here, index = part(from_left, tile, stage), tile * 3 + stage
        copy(here, here, r_send.at[index], r_recv.at[index], x_up).wait_recv()

    def wait_right(tile, stage):
        here, index = part(from_right, tile, stage), tile * 3 + stage
        copy(here, here, l_send.at[index], l_recv.at[index], x_down).wait_recv()

    def first_sends(tile):
        at = tile * 3 * pairs

        @pl.loop(0, pairs)
        def _(i):
            to_right[at + i] = first_block(tile, d_far, 0, i).astype(dtype)

        send_right(tile, 0).start()

        @pl.loop(0, pairs)
        def _(i):
            to_left[at + i] = first_block(tile, d_far, half_c, i).astype(dtype)

        send_left(tile, 0).start()

        @pl.loop(0, pairs)
        def _(i):
            to_right[at + pairs + i] = first_block(tile, d_right, half_c, i).astype(dtype)

        send_right(tile, 1).start()

        @pl.loop(0, pairs)
        def _(i):
            to_left[at + pairs + i] = first_block(tile, d_left, 0, i).astype(dtype)

        send_left(tile, 1).start()

    def pass_sums(tile):
        at = tile * 3 * pairs
        wait_left(tile, 0)

        @pl.loop(0, pairs)
        def _(i):
            total = first_block(tile, d_right, 0, i) + from_left[at + i].astype(F32)
            to_right[at + 2 * pairs + i] = total.astype(dtype)

        send_right(tile, 2).start()
        wait_right(tile, 0)

        @pl.loop(0, pairs)
        def _(i):
            total = first_block(tile, d_left, half_c, i) + from_right[at + i].astype(F32)
            to_left[at + 2 * pairs + i] = total.astype(dtype)

        send_left(tile, 2).start()

    def first_results(rr):
        tiles = (rr, 2 + rr)
        rows = slice(rr * half, (rr + 1) * half)
        for tile in tiles:
            for stage in (1, 2):
                wait_right(tile, stage)
                wait_left(tile, stage)
        for base, left_stage, right_stage in ((0, 2, 1), (half_c, 1, 2)):

            @pl.loop(0, pairs)
            def _(i):
                one, two = [
                    first_block(tile, dep, base, i)
                    + from_left[(tile * 3 + left_stage) * pairs + i].astype(F32)
                    + from_right[(tile * 3 + right_stage) * pairs + i].astype(F32)
                    for tile in tiles
                ]
                result[base + i, rows, 0:half] = jnp.where(low_lanes, one, pltpu.roll(two, quarter, 1)).astype(dtype)
                result[base + pairs + i, rows, 0:half] = jnp.where(
                    low_lanes, pltpu.roll(one, quarter, 1), two
                ).astype(dtype)

    def packed(rr, dest, u):
        return folded((own_prod[rr], ids1), (pair_prod[rr], ids2), dest, u, half_c + u)

    def second_part(refs, rr, stage, k, stages):
        return refs.at[pl.ds((rr * stages + stage) * half_c + k * pairs, pairs)]

    def send_mirror(rr, stage, k):
        index = (rr * 2 + stage) * 2 + k
        return copy(
            second_part(to_mirror, rr, stage, k, 2), second_part(from_mirror, rr, stage, k, 2),
            m_send.at[index], m_recv.at[index], mirror,
        )

    def send_pair(rr, k):
        index = rr * 2 + k
        return copy(
            second_part(to_pair, rr, 0, k, 1), second_part(from_pair, rr, 0, k, 1),
            p_send.at[index], p_recv.at[index], pair,
        )

    def second_sends(rr, stage):
        dest = (d_far, d_mirror)[stage]
        for k in range(2):

            @pl.loop(0, pairs)
            def _(i):
                u = k * pairs + i
                to_mirror[(rr * 2 + stage) * half_c + u] = packed(rr, dest, u).astype(dtype)

            send_mirror(rr, stage, k).start()

    def second_sums(rr):
        for k in range(2):
            send_mirror(rr, 0, k).wait_recv()

            @pl.loop(0, pairs)
            def _(i):
                u = k * pairs + i
                total = packed(rr, d_pair, u) + from_mirror[rr * 2 * half_c + u].astype(F32)
                to_pair[rr * half_c + u] = total.astype(dtype)

            send_pair(rr, k).start()

    def write(rr, k):
        rows = pl.ds(rr * half, half)
        return [
            pltpu.make_async_copy(
                result.at[pl.ds(first + k * pairs, pairs), rows], out_hbm.at[pl.ds(first + k * pairs, pairs), rows],
                out_sem.at[(rr * 2 + k) * 2 + number],
            )
            for number, first in enumerate((0, half_c))
        ]

    def second_results(rr):
        rows = slice(rr * half, (rr + 1) * half)
        for k in range(2):
            send_pair(rr, k).wait_recv()
            send_mirror(rr, 1, k).wait_recv()

            @pl.loop(0, pairs)
            def _(i):
                u = k * pairs + i
                mine = packed(rr, dep, u) + from_mirror[(rr * 2 + 1) * half_c + u].astype(F32)
                other = from_pair[rr * half_c + u].astype(F32)
                low = jnp.where(side == 0, mine, other)
                high = jnp.where(side == 0, other, mine)
                result[u, rows, half : 2 * half] = jnp.where(low_lanes, low, pltpu.roll(high, quarter, 1)).astype(dtype)
                result[half_c + u, rows, half : 2 * half] = jnp.where(
                    low_lanes, pltpu.roll(low, quarter, 1), high
                ).astype(dtype)

            for made in write(rr, k):
                made.start()

    forward_b(0, unit_one[0])
    forward_b(0, unit_one[1])
    forward_b(0, unit_one[2])
    forward_meta(0)
    pack(0)
    across_a(a_own, 0, 0)
    send_first(b_unit(z, core, unit_two[0]), unit_two[0])
    send_first(b_unit(z, core, unit_two[2]), unit_two[2])
    forward_meta(1)
    send_first(b_unit(z, core, unit_two[1]), unit_two[1])
    forward_b(0, unit_two[0])
    forward_meta(2)
    forward_b(1, unit_one[1])
    forward_b(1, unit_one[2])
    pack(1)
    send_own_a(1)
    forward_b(0, unit_two[2])
    forward_meta(3)
    forward_b(1, unit_one[0])
    forward_b(0, unit_two[1])
    forward_b(2, unit_one[1])
    rest_a(a_own, 0, 0)
    send_raw_a(1)
    forward_b(1, unit_two[0])
    forward_b(2, unit_one[2])
    forward_b(2, unit_one[0])
    pair_tables()
    table1 = plan(0, tab_int1, tab_scale1, ids1, scales1, 3)
    forward_b(3, unit_one[1])
    send_first(b_unit(z, core, unit_second[0]), unit_second[0])
    forward_b(1, unit_two[2])
    forward_b(3, unit_one[2])
    forward_b(1, unit_two[1])
    across_a(a_own, 1, 0)
    finish(unit_one[1])
    forward_b(2, unit_two[0])
    forward_b(3, unit_one[0])
    for made in table1 + local:
        made.wait()
    finish(unit_one[2])
    send_first(b_unit(z, core, unit_second[1]), unit_second[1])
    spread_pair_a(0)
    finish(unit_one[0])
    multiply(a_own[0], b_one, ids1, scales1, prod0, True)
    first_sends(0)
    forward_b(2, unit_two[1])
    forward_b(2, unit_two[2])
    spread_pair_a(1)
    forward_b(0, unit_second[0])
    rest_a(a_own, 1, 0)
    multiply(a_own[1], b_one, ids1, scales1, prod1, True)
    first_sends(1)
    forward_b(3, unit_two[2])
    finish(unit_two[2])
    pass_sums(0)
    forward_b(3, unit_two[0])
    forward_b(0, unit_second[1])
    forward_b(3, unit_two[1])
    finish(unit_two[0])
    forward_b(1, unit_second[0])
    finish(unit_two[1])
    multiply(a_own[1], b_two, ids1, scales1, prod3, True)
    first_sends(3)
    across_a(a_pair, 0, 6)
    forward_b(1, unit_second[1])
    multiply(a_own[0], b_two, ids1, scales1, prod2, True)
    forward_b(2, unit_second[0])
    first_sends(2)
    pass_sums(1)
    forward_b(2, unit_second[1])
    pulled(meta_y.at[1], meta_send.at[pair_meta], meta_recv.at[pair_meta])
    pulled(meta_z.at[1], meta_send.at[pair_meta + 1], meta_recv.at[pair_meta + 1])
    table2 = plan(1, tab_int2, tab_scale2, ids2, scales2, 5)
    pass_sums(3)
    across_a(a_pair, 1, 6)
    forward_b(3, unit_second[0])
    forward_b(3, unit_second[1])
    finish(unit_second[0])
    for made in table2:
        made.wait()
    finish(unit_second[1])
    multiply(a_own[0], b_second, ids1, scales1, prod4, False)
    rest_a(a_pair, 0, 6)
    pass_sums(2)
    multiply(a_pair[0], b_second, ids2, scales2, prod6, False)
    rest_a(a_pair, 1, 6)
    second_sends(0, 0)
    first_results(1)
    second_sends(0, 1)
    multiply(a_pair[1], b_second, ids2, scales2, prod7, False)
    multiply(a_own[1], b_second, ids1, scales1, prod5, False)
    second_sums(0)
    second_sends(1, 0)
    second_sends(1, 1)
    first_results(0)
    second_sums(1)
    second_results(0)
    second_results(1)

    for rr in range(2):
        for k in range(2):
            for made in write(rr, k):
                made.wait()
            send_pair(rr, k).wait_send()
            for stage in range(2):
                send_mirror(rr, stage, k).wait_send()
    for tile in range(4):
        for stage in range(3):
            send_right(tile, stage).wait_send()
            send_left(tile, stage).wait_send()

    for made in sends:
        made.wait_send()


def shards(a_blocks, a_scale, a_rows, a_cols, b_blocks, b_scale, b_cols, c_rows, c_cols):
    edge = a_blocks.shape[1]
    half = edge // 2
    a_cap, c_cap = a_blocks.shape[0], c_rows.shape[0]
    per, kb = b_blocks.shape[0], b_blocks.shape[3]
    n_r, n_y, n_x = lax.axis_size("row"), lax.axis_size("col"), lax.axis_size("depth")
    dims = (n_x, n_y, n_r, a_cap, per, kb, c_cap)
    n_c = n_y * a_cap
    half_c = c_cap // 2

    width = -(-kb * n_c // LANES) * LANES

    dtype = a_blocks.dtype
    block, part = (edge, edge), (edge, half)
    dma = pltpu.SemaphoreType.DMA
    hops = n_r // 4
    n_meta = (n_y - 1) + (n_x - 1) + 1 + 4 * hops + 2
    n_units = 2 * kb + per
    n_ring = 2 * hops * n_units
    rows = (half, edge)
    tile = (half, half)
    any_space = pl.BlockSpec(memory_space=pl.ANY)
    vmem = pl.BlockSpec(memory_space=pltpu.VMEM)
    return pl.pallas_call(
        functools.partial(kernel, dims),
        out_shape=jax.ShapeDtypeStruct((c_cap,) + block, dtype),
        in_specs=[any_space, any_space] + [vmem] * 7,
        out_specs=any_space,
        scratch_shapes=[pltpu.VMEM((n_c,) + rows, dtype)] * 4
        + [
            pltpu.VMEM((n_r * kb,) + part, dtype),
            pltpu.VMEM((n_r * kb,) + part, dtype),
            pltpu.VMEM((n_r * per * kb,) + part, dtype),
            pltpu.VMEM((per, kb) + block, dtype),
            pltpu.VMEM((per, kb) + part, dtype),
            pltpu.VMEM((8, LANES), F32),
            pltpu.VMEM((n_x, 8, LANES), F32),
            pltpu.VMEM((2, n_y, 8, LANES), F32),
            pltpu.VMEM((2, n_r, 8, LANES), F32),
        ]
        + [
            space((8, width), kind)
            for _ in range(2)
            for space in (pltpu.VMEM, pltpu.SMEM)
            for kind in (jnp.int32, F32)
        ]
        + [pltpu.VMEM(tile, F32)]
        + [pltpu.VMEM((kb * n_c + 1,) + tile, dtype)] * 8
        + [pltpu.VMEM((12 * (half_c // 2),) + tile, dtype)] * 4
        + [pltpu.VMEM((4 * half_c,) + tile, dtype)] * 2
        + [pltpu.VMEM((2 * half_c,) + tile, dtype)] * 2
        + [
            pltpu.VMEM((c_cap,) + block, dtype),
            dma((7,)),
            dma((n_meta,)),
            dma((n_meta,)),
            dma((n_ring,)),
            dma((n_ring,)),
            dma((n_units + n_ring,)),
            dma((n_units + n_ring,)),
            dma((per,)),
            dma((per,)),
            dma((28,)),
            dma((28,)),
        ]
        + [dma((12,))] * 4
        + [dma((8,))] * 2
        + [dma((4,))] * 2
        + [dma((8,))],
        compiler_params=pltpu.CompilerParams(
            collective_id=0, has_side_effects=True, vmem_limit_bytes=62 * 1024 * 1024
        ),
    )(
        a_blocks,
        b_blocks.reshape(per, kb, edge, edge),
        a_scale.reshape(1, a_cap),
        a_rows.reshape(1, a_cap),
        a_cols.reshape(1, a_cap),
        b_scale.reshape(per, kb),
        b_cols.reshape(per, kb),
        c_rows.reshape(1, c_cap),
        c_cols.reshape(1, c_cap),
    )


def solution(mesh):
    return jax.shard_map(
        shards,
        mesh=mesh,
        in_specs=(
            P(("row", "col", "depth"), None, None),
            P(("row", "col", "depth")),
            P(("row", "col", "depth")),
            P(("row", "col", "depth")),
            P("row", "col", "depth", None, None, None),
            P("row", "col", "depth", None),
            P("row", "col", "depth", None),
            P(("row", "col", "depth")),
            P(("row", "col", "depth")),
        ),
        out_specs=P(("row", "col", "depth"), None, None),
        check_vma=False,
    )
```

```python
import functools

import jax
import jax.numpy as jnp
from jax import lax
from jax.experimental import pallas as pl
from jax.experimental.pallas import tpu as pltpu
from jax.sharding import PartitionSpec as P

MESH = pl.DeviceIdType.MESH
LANES = 128
ROW_KEY = 1024.0
F32 = jnp.float32


def iota(shape, dim):
    return lax.broadcasted_iota(jnp.int32, shape, dim)


def schedule(dims, kind, meta_x, meta_y, meta_z, tab_int, tab_scale):
    n_x, n_y, n_r, a_cap, per, kb, c_cap = dims
    n_a = n_y * a_cap
    n_g = n_r * per
    n_slots = n_x * c_cap
    eye = iota((a_cap, LANES), 0) == iota((a_cap, LANES), 1)
    lane = iota((n_a, LANES), 1)

    def column(which):
        parts = [
            jnp.sum(jnp.where(eye, meta_y[kind, c, which : which + 1, :], 0.0), axis=1, keepdims=True)
            for c in range(n_y)
        ]
        return jnp.concatenate(parts, axis=0)

    a_scale, a_rows, a_cols = column(0), column(1), column(2)
    group = a_cols.astype(jnp.int32) // n_x
    b_scale = jnp.zeros((n_a, LANES), F32)
    b_cols = jnp.zeros((n_a, LANES), F32)
    for g in range(n_g):
        here = group == g
        d, i = g // per, g % per
        b_scale = jnp.where(here, meta_z[kind, d, 3 + i : 4 + i, :], b_scale)
        b_cols = jnp.where(here, meta_z[kind, d, 5 + i : 6 + i, :], b_cols)
    device, inner = group // per, group % per
    slots, weights, b_ids, first_ids = [], [], [], []
    for t in range(kb):
        col = jnp.sum(jnp.where(lane == t, b_cols, 0.0), axis=1, keepdims=True)
        scale = jnp.sum(jnp.where(lane == t, b_scale, 0.0), axis=1, keepdims=True)
        key = a_rows * ROW_KEY + col
        found = jnp.zeros((n_a, LANES), F32)
        for e in range(n_x):
            hit = (key == meta_x[e, 7:8, :]) & (lane < c_cap)
            found = jnp.where(hit, (lane + (e * c_cap + 1)).astype(F32), found)
        slot = jnp.max(found, axis=1, keepdims=True)
        slots.append(jnp.where(slot > 0, slot - 1, float(n_slots)))
        weights.append(a_scale * scale)
        b_ids.append((group * kb + t).astype(F32))
        first_ids.append((device * kb + t).astype(F32))
    slot, weight = jnp.concatenate(slots, axis=0), jnp.concatenate(weights, axis=0)
    a_id = jnp.concatenate([iota((n_a, 1), 0).astype(F32)] * kb, axis=0)
    b_id, first_id = jnp.concatenate(b_ids, axis=0), jnp.concatenate(first_ids, axis=0)
    low = jnp.where(jnp.concatenate([inner] * kb, axis=0) == 0, weight, 0.0)
    n_p = kb * n_a
    width = tab_int.shape[1]
    place, lane = iota((n_p, width), 0), iota((n_p, width), 1)
    row_slot = jnp.sum(jnp.where(place == lane, slot, 0.0), axis=0, keepdims=True)
    row_slot = jnp.where(lane[:1] < n_p, row_slot, 1e6)
    earlier = (row_slot == slot) & (lane < place)
    before = (row_slot < slot) | earlier
    rank = jnp.sum(jnp.where(before, 1.0, 0.0), axis=1, keepdims=True)
    keep = jnp.where(jnp.sum(jnp.where(earlier, 1.0, 0.0), axis=1, keepdims=True) > 0, 1.0, 0.0)
    lane_f = lane.astype(F32)
    mine = rank == lane_f

    def ordered(values):
        return jnp.sum(jnp.where(mine, values, 0.0), axis=0, keepdims=True)

    last = jnp.sum(jnp.where(slot <= lane_f, 1.0, 0.0), axis=0, keepdims=True) - 1.0
    some = jnp.sum(jnp.where(slot == lane_f, 1.0, 0.0), axis=0, keepdims=True)
    last = jnp.where(some > 0, last, float(n_p))
    zero = jnp.zeros((1, width), F32)
    table = jnp.concatenate(
        [ordered(a_id), ordered(b_id), last, ordered(first_id), zero, zero, zero, zero], axis=0
    ).astype(jnp.int32)
    which = iota(table.shape, 0)
    top = jnp.where(which == 0, n_a - 1, jnp.where(which == 1, n_g * kb - 1, n_p))
    top = jnp.where(which == 3, n_r * kb - 1, top)
    tab_int[...] = jnp.clip(table, 0, top)
    tab_scale[...] = jnp.concatenate(
        [ordered(weight), ordered(keep), ordered(low), ordered(weight - low), zero, zero, zero, zero], axis=0
    )


def kernel(
    dims, a_hbm, b_hbm, *rest):
    small, (out_hbm,), scratch = rest[:7], rest[7:8], rest[8:]
    body(dims, a_hbm, b_hbm, small, out_hbm, scratch[:7], *scratch[7:])


def body(
    dims, a_hbm, b_hbm, small, out_hbm, tables,
    a_own0, a_own1, a_pair0, a_pair1, b_one, b_two, b_second, raw_own, raw_pair, meta, meta_x, meta_y, meta_z,
    tab_int1, tab_scale1, ids1, scales1, tab_int2, tab_scale2, ids2, scales2,
    acc, prod0, prod1, prod2, prod3, own_first,
    to_right, to_left, from_left, from_right, to_mirror, from_mirror, to_pair, from_pair, result,
    local_sem, meta_send, meta_recv, ring_send, ring_recv, core_send, core_recv, raw_send, raw_recv, a_send, a_recv,
    r_send, r_recv, l_send, l_recv, m_send, m_recv, p_send, p_recv, out_sem, small_sem,
):
    n_x, n_y, n_r, a_cap, per, kb, c_cap = dims
    n_z = n_r // 2
    n_g = n_r * per
    n_c = n_y * a_cap
    half = b_second.shape[2]
    quarter = half // 2
    a_own, a_pair = (a_own0, a_own1), (a_pair0, a_pair1)
    first_prod = ((prod0, prod1), (prod2, prod3))
    own_prod, pair_prod = (prod0, prod1), (prod2, prod3)
    row, col, dep = lax.axis_index("row"), lax.axis_index("col"), lax.axis_index("depth")
    z, core = row // 2, row % 2

    def at_z(step):
        return (lax.rem(z + step + n_z, n_z) * 2 + core, col, dep)

    def at_y(step):
        return (row, lax.rem(col + step + n_y, n_y), dep)

    def at_x(step):
        return (row, col, lax.rem(dep + step + n_x, n_x))

    sibling = (z * 2 + 1 - core, col, dep)
    d_pair, d_mirror, d_far = dep + 1 - 2 * (dep % 2), n_x - 1 - dep, lax.rem(dep + 2, n_x)
    pair, mirror = (row, col, d_pair), (row, col, d_mirror)
    side = ((dep + 1) // 2) % 2
    second_cols = pl.ds(half, half)
    low_lanes = iota((1, half), 1) < quarter

    local_raw = pltpu.make_async_copy(b_hbm, raw_own, local_sem.at[0])
    local_raw.start()
    loads = [pltpu.make_async_copy(src, dst, small_sem.at[i]) for i, (src, dst) in enumerate(zip(small, tables))]
    for made in loads:
        made.start()
    a_scale, a_rows, a_cols, b_scale, b_cols, c_rows, c_cols = tables

    meta[...] = jnp.zeros_like(meta)
    for made in loads:
        made.wait()
    meta[0:1, 0:a_cap] = a_scale[...]
    meta[1:2, 0:a_cap] = a_rows[...].astype(F32)
    meta[2:3, 0:a_cap] = a_cols[...].astype(F32)
    meta[3 : 3 + per, 0:kb] = b_scale[...]
    meta[5 : 5 + per, 0:kb] = b_cols[...].astype(F32)
    meta[7:8, 0:c_cap] = c_rows[...].astype(F32) * ROW_KEY + c_cols[...].astype(F32)

    barrier = pltpu.get_barrier_semaphore()
    partners = [sibling, at_z(1), at_z(-1)] + [at_y(j) for j in range(1, n_y)] + [at_x(j) for j in range(1, n_x)]
    for partner in partners:
        pl.semaphore_signal(barrier, inc=1, device_id=partner, device_id_type=MESH)
    local_raw.wait()

    def pack_first(refs, number):
        for t in range(kb):
            one, two = raw_own[0, t, :, 0:half].astype(F32), raw_own[1, t, :, 0:half].astype(F32)
            one = pltpu.roll(one, quarter, 1) if number else one
            two = two if number else pltpu.roll(two, quarter, 1)
            refs[row * kb + t] = jnp.where(low_lanes, one, two).astype(refs.dtype)

    pack_first(b_one, 0)
    pl.semaphore_wait(barrier, len(partners))

    sends = []

    def copy(src, dst, send, recv, device):
        return pltpu.make_async_remote_copy(
            src_ref=src, dst_ref=dst, send_sem=send, recv_sem=recv, device_id=device, device_id_type=MESH
        )

    def push(src, dst, send, recv, device):
        made = copy(src, dst, send, recv, device)
        made.start()
        sends.append(made)

    def pulled(dst, send, recv):
        copy(dst, dst, send, recv, sibling).wait_recv()

    count = 0
    meta_waits = []
    for j in range(1, n_y):
        push(meta, meta_y.at[0, col], meta_send.at[count], meta_recv.at[count], at_y(j))
        meta_waits.append((meta_y.at[0, lax.rem(col - j + n_y, n_y)], count))
        count += 1
    for j in range(1, n_x):
        push(meta, meta_x.at[dep], meta_send.at[count], meta_recv.at[count], at_x(j))
        meta_waits.append((meta_x.at[lax.rem(dep - j + n_x, n_x)], count))
        count += 1
    push(meta, meta_z.at[0, row], meta_send.at[count], meta_recv.at[count], sibling)
    meta_waits.append((meta_z.at[0, z * 2 + 1 - core], count))
    count += 1
    hops_up, hops_down = n_z // 2, (n_z - 1) // 2
    ring_meta = count
    push(meta, meta_z.at[0, row], meta_send.at[count], meta_recv.at[count], at_z(1))
    push(meta, meta_z.at[0, row], meta_send.at[count + 1], meta_recv.at[count + 1], at_z(-1))
    count += 2 * hops_up
    core_meta = count
    count += 2 * hops_up
    pair_meta = count

    up, down = at_z(1), at_z(-1)
    units = [(b_one, kb, t, 1, t // 2) for t in range(kb)]
    units += [(b_two, kb, t, 1, 1 - t // 2) for t in range(kb)]
    units += [(b_second, per * kb, inner * kb, kb, inner) for inner in range(per)]
    n_u = len(units)
    unit_one, unit_two = list(range(kb)), list(range(kb, 2 * kb))
    unit_second = list(range(2 * kb, 2 * kb + per))

    def b_unit(origin_z, origin_core, unit):
        refs, each, first, size, _ = units[unit]
        return refs.at[pl.ds((origin_z * 2 + origin_core) * each + first, size)]

    def a_part(refs, origin, first):
        return refs.at[pl.ds(origin * a_cap + first, a_cap // 2)]

    def ring_slot(direction, step, unit):
        return (direction * hops_up + step) * n_u + unit

    def hops(direction, unit):
        return hops_up if units[unit][4] == direction else hops_down

    def send_first(src, unit):
        for direction, device in ((0, up), (1, down)):
            index = ring_slot(direction, 0, unit)
            push(src, b_unit(z, core, unit), ring_send.at[index], ring_recv.at[index], device)
        push(src, b_unit(z, core, unit), core_send.at[unit], core_recv.at[unit], sibling)

    for unit in unit_one:
        send_first(b_unit(z, core, unit), unit)
    for inner in range(per):
        push(b_hbm.at[inner, :, :, second_cols], raw_pair.at[inner], raw_send.at[inner], raw_recv.at[inner], pair)

    mid = a_cap // 2
    y_up, y_down = at_y(1), at_y(-1)
    left, right, across = at_y(-1)[1], at_y(1)[1], at_y(2)[1]

    def a_rows_of(rr, first):
        return a_hbm.at[pl.ds(first, mid), pl.ds(rr * half, half)]

    def send_own_a(rr):
        for first, slot, device in ((0, 0, y_up), (mid, 3, y_down), (mid, 1, y_up), (0, 4, y_down)):
            index = rr * 14 + slot
            push(a_rows_of(rr, first), a_part(a_own[rr], col, first), a_send.at[index], a_recv.at[index], device)

    def send_raw_a(rr):
        for number in range(2):
            first, index = number * mid, rr * 14 + 12 + number
            push(a_rows_of(rr, first), a_part(a_pair[rr], col, first), a_send.at[index], a_recv.at[index], pair)

    send_own_a(0)
    send_raw_a(0)
    local = [
        pltpu.make_async_copy(
            a_hbm.at[:, pl.ds(rr * half, half)], a_own[rr].at[pl.ds(col * a_cap, a_cap)], local_sem.at[1 + rr]
        )
        for rr in range(2)
    ]
    for made in local:
        made.start()
    meta_x[dep] = meta[...]
    meta_y[0, col] = meta[...]
    meta_z[0, row] = meta[...]

    def forward_meta(step):
        for direction, limit in ((0, hops_up), (1, hops_down)):
            if step >= limit:
                continue
            origin_z = lax.rem(z - step - 1 + n_z, n_z) if direction == 0 else lax.rem(z + step + 1, n_z)
            here = meta_z.at[0, origin_z * 2 + core]
            index = ring_meta + 2 * step + direction
            pulled(here, meta_send.at[index], meta_recv.at[index])
            if step + 1 < limit:
                push(here, here, meta_send.at[index + 2], meta_recv.at[index + 2], up if direction == 0 else down)
            index = core_meta + 2 * step + direction
            push(here, here, meta_send.at[index], meta_recv.at[index], sibling)
            meta_waits.append((meta_z.at[0, origin_z * 2 + 1 - core], index))

    def pair_tables():
        for here, index in meta_waits:
            pulled(here, meta_send.at[index], meta_recv.at[index])
        push(meta_y.at[0], meta_y.at[1], meta_send.at[pair_meta], meta_recv.at[pair_meta], pair)
        push(meta_z.at[0], meta_z.at[1], meta_send.at[pair_meta + 1], meta_recv.at[pair_meta + 1], pair)

    core_waits = [[(b_unit(z, 1 - core, unit), unit)] for unit in range(n_u)]

    def pack(inner):
        pulled(raw_pair.at[inner], raw_send.at[inner], raw_recv.at[inner])
        base = (row * per + inner) * kb
        for t in range(kb):
            mine, other = raw_own[inner, t, :, half : 2 * half].astype(F32), raw_pair[inner, t].astype(F32)
            mine = jnp.where(side == 0, mine, pltpu.roll(mine, quarter, 1))
            other = jnp.where(side == 0, pltpu.roll(other, quarter, 1), other)
            b_second[base + t] = jnp.where(low_lanes, mine, other).astype(b_second.dtype)

    def forward_b(step, unit):
        for direction in range(2):
            limit = hops(direction, unit)
            if step >= limit:
                continue
            origin_z = lax.rem(z - step - 1 + n_z, n_z) if direction == 0 else lax.rem(z + step + 1, n_z)
            here = b_unit(origin_z, core, unit)
            index = ring_slot(direction, step, unit)
            pulled(here, ring_send.at[index], ring_recv.at[index])
            if step + 1 < limit:
                index = ring_slot(direction, step + 1, unit)
                push(here, here, ring_send.at[index], ring_recv.at[index], up if direction == 0 else down)
            index = n_u + ring_slot(direction, step, unit)
            push(here, here, core_send.at[index], core_recv.at[index], sibling)
            core_waits[unit].append((b_unit(origin_z, 1 - core, unit), index))

    def arrived(refs, rr, origin, first, slot):
        here, index = a_part(refs[rr], origin, first), rr * 14 + slot
        pulled(here, a_send.at[index], a_recv.at[index])
        return here

    def hand_on(here, rr, slot, device):
        index = rr * 14 + slot
        push(here, here, a_send.at[index], a_recv.at[index], device)

    def across_a(refs, rr, base):
        hand_on(arrived(refs, rr, left, 0, base), rr, base + 2, y_up)
        hand_on(arrived(refs, rr, right, mid, base + 3), rr, base + 5, y_down)

    def rest_a(refs, rr, base):
        arrived(refs, rr, left, mid, base + 1)
        arrived(refs, rr, right, 0, base + 4)
        arrived(refs, rr, across, 0, base + 2)
        arrived(refs, rr, across, mid, base + 5)

    def spread_pair_a(rr):
        low_a, high_a = arrived(a_pair, rr, col, 0, 12), arrived(a_pair, rr, col, mid, 13)
        hand_on(low_a, rr, 6, y_up)
        hand_on(high_a, rr, 9, y_down)
        hand_on(high_a, rr, 7, y_up)
        hand_on(low_a, rr, 10, y_down)

    def finish(unit):
        for here, index in core_waits[unit]:
            pulled(here, core_send.at[index], core_recv.at[index])

    def plan(kind, tab_int, tab_scale, ids, scales, sem):
        schedule(dims, kind, meta_x, meta_y, meta_z, tab_int, tab_scale)
        made = [
            pltpu.make_async_copy(tab_int, ids, local_sem.at[sem]),
            pltpu.make_async_copy(tab_scale, scales, local_sem.at[sem + 1]),
        ]
        for one in made:
            one.start()
        return made

    def bounded(index, size):
        return jnp.clip(index, 0, size - 1)

    def multiply(a_refs, b_refs, ids, scales, prod, split):
        n_p = kb * n_c
        acc[...] = jnp.zeros_like(acc)
        prod[n_p] = jnp.zeros(prod.shape[1:], prod.dtype)

        @pl.loop(0, n_p, unroll=16)
        def _(j):
            left_block = a_refs[bounded(ids[0, j], n_c)]
            right_block = b_refs[bounded(ids[3 if split else 1, j], b_refs.shape[0])]
            product = jnp.dot(left_block, right_block, preferred_element_type=F32)
            weight = jnp.where(low_lanes, scales[2, j], scales[3, j]) if split else scales[0, j]
            total = acc[...] * scales[1, j] + product * weight
            acc[...] = total
            prod[j] = total.astype(prod.dtype)

    def folded(mine, other, dest, u, v):
        def take(which, index):
            prod, ids = which
            return prod[bounded(ids[2, dest * c_cap + index], prod.shape[0])].astype(F32)

        straight = jnp.where(low_lanes, take(mine, u), take(other, v))
        crossed = jnp.where(low_lanes, take(mine, v), take(other, u))
        return straight + pltpu.roll(crossed, quarter, 1)

    half_c = c_cap // 2
    pairs = half_c // 2
    x_up, x_down = at_x(1), at_x(-1)
    d_right, d_left = x_up[2], x_down[2]
    dtype = result.dtype

    def first_block(tile, dest, base, i):
        both = (first_prod[tile // 2][tile % 2], ids1)
        return folded(both, both, dest, base + i, base + pairs + i)

    def part(refs, tile, stage):
        return refs.at[pl.ds((tile * 3 + stage) * pairs, pairs)]

    def send_right(tile, stage):
        index = tile * 3 + stage
        return copy(part(to_right, tile, stage), part(from_left, tile, stage), r_send.at[index], r_recv.at[index], x_up)

    def send_left(tile, stage):
        index = tile * 3 + stage
        return copy(part(to_left, tile, stage), part(from_right, tile, stage), l_send.at[index], l_recv.at[index], x_down)

    def wait_left(tile, stage):
        here, index = part(from_left, tile, stage), tile * 3 + stage
        copy(here, here, r_send.at[index], r_recv.at[index], x_up).wait_recv()

    def wait_right(tile, stage):
        here, index = part(from_right, tile, stage), tile * 3 + stage
        copy(here, here, l_send.at[index], l_recv.at[index], x_down).wait_recv()

    def first_sends(tile):
        at = tile * 3 * pairs

        @pl.loop(0, pairs)
        def _(i):
            to_right[at + i] = first_block(tile, d_far, 0, i).astype(dtype)

        send_right(tile, 0).start()

        @pl.loop(0, pairs)
        def _(i):
            to_left[at + i] = first_block(tile, d_far, half_c, i).astype(dtype)

        send_left(tile, 0).start()

        @pl.loop(0, pairs)
        def _(i):
            to_right[at + pairs + i] = first_block(tile, d_right, half_c, i).astype(dtype)

        send_right(tile, 1).start()

        @pl.loop(0, pairs)
        def _(i):
            to_left[at + pairs + i] = first_block(tile, d_left, 0, i).astype(dtype)

        send_left(tile, 1).start()

    def pass_sums(tile):
        at = tile * 3 * pairs
        wait_left(tile, 0)

        @pl.loop(0, pairs)
        def _(i):
            total = first_block(tile, d_right, 0, i) + from_left[at + i].astype(F32)
            to_right[at + 2 * pairs + i] = total.astype(dtype)

        send_right(tile, 2).start()
        wait_right(tile, 0)

        @pl.loop(0, pairs)
        def _(i):
            total = first_block(tile, d_left, half_c, i) + from_right[at + i].astype(F32)
            to_left[at + 2 * pairs + i] = total.astype(dtype)

        send_left(tile, 2).start()

    def keep_own(tile):
        @pl.loop(0, pairs)
        def _(i):
            own_first[tile * half_c + i] = first_block(tile, dep, 0, i)
            own_first[tile * half_c + pairs + i] = first_block(tile, dep, half_c, i)

    def first_results(rr):
        tiles = (rr, 2 + rr)
        rows = slice(rr * half, (rr + 1) * half)
        for tile in tiles:
            for stage in (1, 2):
                wait_right(tile, stage)
                wait_left(tile, stage)
        for base, kept, left_stage, right_stage in ((0, 0, 2, 1), (half_c, pairs, 1, 2)):

            @pl.loop(0, pairs)
            def _(i):
                one, two = [
                    own_first[tile * half_c + kept + i]
                    + from_left[(tile * 3 + left_stage) * pairs + i].astype(F32)
                    + from_right[(tile * 3 + right_stage) * pairs + i].astype(F32)
                    for tile in tiles
                ]
                result[base + i, rows, 0:half] = jnp.where(low_lanes, one, pltpu.roll(two, quarter, 1)).astype(dtype)
                result[base + pairs + i, rows, 0:half] = jnp.where(
                    low_lanes, pltpu.roll(one, quarter, 1), two
                ).astype(dtype)

    def packed(rr, dest, u):
        return folded((own_prod[rr], ids1), (pair_prod[rr], ids2), dest, u, half_c + u)

    def second_part(refs, rr, stage, k, stages):
        return refs.at[pl.ds((rr * stages + stage) * half_c + k * pairs, pairs)]

    def send_mirror(rr, stage, k):
        index = (rr * 2 + stage) * 2 + k
        return copy(
            second_part(to_mirror, rr, stage, k, 2), second_part(from_mirror, rr, stage, k, 2),
            m_send.at[index], m_recv.at[index], mirror,
        )

    def send_pair(rr, k):
        index = rr * 2 + k
        return copy(
            second_part(to_pair, rr, 0, k, 1), second_part(from_pair, rr, 0, k, 1),
            p_send.at[index], p_recv.at[index], pair,
        )

    def second_sends(rr, stage):
        dest = (d_far, d_mirror)[stage]
        for k in range(2):

            @pl.loop(0, pairs)
            def _(i):
                u = k * pairs + i
                to_mirror[(rr * 2 + stage) * half_c + u] = packed(rr, dest, u).astype(dtype)

            send_mirror(rr, stage, k).start()

    def second_sums(rr):
        for k in range(2):
            send_mirror(rr, 0, k).wait_recv()

            @pl.loop(0, pairs)
            def _(i):
                u = k * pairs + i
                total = packed(rr, d_pair, u) + from_mirror[rr * 2 * half_c + u].astype(F32)
                to_pair[rr * half_c + u] = total.astype(dtype)

            send_pair(rr, k).start()

    def write(rr, k):
        rows = pl.ds(rr * half, half)
        return [
            pltpu.make_async_copy(
                result.at[pl.ds(first + k * pairs, pairs), rows], out_hbm.at[pl.ds(first + k * pairs, pairs), rows],
                out_sem.at[(rr * 2 + k) * 2 + number],
            )
            for number, first in enumerate((0, half_c))
        ]

    def second_results(rr):
        rows = slice(rr * half, (rr + 1) * half)
        for k in range(2):
            send_pair(rr, k).wait_recv()
            send_mirror(rr, 1, k).wait_recv()

            @pl.loop(0, pairs)
            def _(i):
                u = k * pairs + i
                mine = packed(rr, dep, u) + from_mirror[(rr * 2 + 1) * half_c + u].astype(F32)
                other = from_pair[rr * half_c + u].astype(F32)
                low = jnp.where(side == 0, mine, other)
                high = jnp.where(side == 0, other, mine)
                result[u, rows, half : 2 * half] = jnp.where(low_lanes, low, pltpu.roll(high, quarter, 1)).astype(dtype)
                result[half_c + u, rows, half : 2 * half] = jnp.where(
                    low_lanes, pltpu.roll(low, quarter, 1), high
                ).astype(dtype)

            for made in write(rr, k):
                made.start()

    forward_meta(0)
    pack_first(b_two, 1)
    send_first(b_unit(z, core, unit_two[1]), unit_two[1])
    forward_b(0, unit_one[0])
    forward_b(0, unit_one[2])
    forward_b(0, unit_one[1])
    forward_b(1, unit_one[0])
    forward_b(1, unit_one[2])
    across_a(a_own, 0, 0)
    send_first(b_unit(z, core, unit_two[0]), unit_two[0])
    forward_meta(1)
    send_first(b_unit(z, core, unit_two[2]), unit_two[2])
    send_own_a(1)
    pack(1)
    send_raw_a(1)
    forward_b(1, unit_one[1])
    forward_b(2, unit_one[2])
    forward_b(0, unit_two[0])
    forward_meta(2)
    forward_b(2, unit_one[0])
    forward_b(2, unit_one[1])
    forward_b(0, unit_two[1])
    forward_b(0, unit_two[2])
    forward_b(3, unit_one[0])
    forward_meta(3)
    pair_tables()
    forward_b(1, unit_two[0])
    forward_b(3, unit_one[1])
    pack(0)
    table1 = plan(0, tab_int1, tab_scale1, ids1, scales1, 3)
    send_first(b_unit(z, core, unit_second[0]), unit_second[0])
    rest_a(a_own, 0, 0)
    forward_b(1, unit_two[2])
    forward_b(3, unit_one[2])
    finish(unit_one[1])
    forward_b(1, unit_two[1])
    forward_b(2, unit_two[0])
    across_a(a_own, 1, 0)
    finish(unit_one[0])
    finish(unit_one[2])
    for made in table1 + local:
        made.wait()
    send_first(b_unit(z, core, unit_second[1]), unit_second[1])
    multiply(a_own[0], b_one, ids1, scales1, prod0, True)
    first_sends(0)
    spread_pair_a(1)
    spread_pair_a(0)
    forward_b(2, unit_two[2])
    forward_b(2, unit_two[1])
    forward_b(0, unit_second[0])
    rest_a(a_own, 1, 0)
    multiply(a_own[1], b_one, ids1, scales1, prod1, True)
    first_sends(1)
    forward_b(0, unit_second[1])
    forward_b(3, unit_two[2])
    pass_sums(0)
    forward_b(3, unit_two[0])
    finish(unit_two[0])
    forward_b(3, unit_two[1])
    across_a(a_pair, 1, 6)
    keep_own(1)
    pulled(meta_y.at[1], meta_send.at[pair_meta], meta_recv.at[pair_meta])
    pulled(meta_z.at[1], meta_send.at[pair_meta + 1], meta_recv.at[pair_meta + 1])
    table2 = plan(1, tab_int2, tab_scale2, ids2, scales2, 5)
    forward_b(1, unit_second[0])
    pass_sums(1)
    finish(unit_two[2])
    finish(unit_two[1])
    forward_b(1, unit_second[1])
    multiply(a_own[0], b_two, ids1, scales1, prod2, True)
    first_sends(2)
    across_a(a_pair, 0, 6)
    multiply(a_own[1], b_two, ids1, scales1, prod3, True)
    forward_b(2, unit_second[1])
    keep_own(0)
    forward_b(2, unit_second[0])
    first_sends(3)
    keep_own(3)
    forward_b(3, unit_second[1])
    rest_a(a_pair, 1, 6)
    pass_sums(2)
    finish(unit_second[1])
    forward_b(3, unit_second[0])
    pass_sums(3)
    for made in table2:
        made.wait()
    finish(unit_second[0])
    multiply(a_own[1], b_second, ids1, scales1, prod1, False)
    multiply(a_pair[1], b_second, ids2, scales2, prod3, False)
    second_sends(1, 0)
    second_sends(1, 1)
    keep_own(2)
    rest_a(a_pair, 0, 6)
    multiply(a_pair[0], b_second, ids2, scales2, prod2, False)
    multiply(a_own[0], b_second, ids1, scales1, prod0, False)
    second_sends(0, 0)
    second_sends(0, 1)
    first_results(0)
    second_sums(1)
    second_sums(0)
    first_results(1)
    second_results(1)
    second_results(0)

    for rr in range(2):
        for k in range(2):
            for made in write(rr, k):
                made.wait()
            send_pair(rr, k).wait_send()
            for stage in range(2):
                send_mirror(rr, stage, k).wait_send()
    for tile in range(4):
        for stage in range(3):
            send_right(tile, stage).wait_send()
            send_left(tile, stage).wait_send()

    for made in sends:
        made.wait_send()


def shards(a_blocks, a_scale, a_rows, a_cols, b_blocks, b_scale, b_cols, c_rows, c_cols):
    edge = a_blocks.shape[1]
    half = edge // 2
    a_cap, c_cap = a_blocks.shape[0], c_rows.shape[0]
    per, kb = b_blocks.shape[0], b_blocks.shape[3]
    n_r, n_y, n_x = lax.axis_size("row"), lax.axis_size("col"), lax.axis_size("depth")
    dims = (n_x, n_y, n_r, a_cap, per, kb, c_cap)
    n_c = n_y * a_cap
    half_c = c_cap // 2

    width = -(-kb * n_c // LANES) * LANES

    dtype = a_blocks.dtype
    block, part = (edge, edge), (edge, half)
    dma = pltpu.SemaphoreType.DMA
    hops = n_r // 4
    n_meta = (n_y - 1) + (n_x - 1) + 1 + 4 * hops + 2
    n_units = 2 * kb + per
    n_ring = 2 * hops * n_units
    rows = (half, edge)
    tile = (half, half)
    any_space = pl.BlockSpec(memory_space=pl.ANY)
    small = [v.reshape(1, a_cap) for v in (a_scale, a_rows, a_cols)]
    small += [v.reshape(per, kb) for v in (b_scale, b_cols)]
    small += [v.reshape(1, c_cap) for v in (c_rows, c_cols)]
    gathered = pl.pallas_call(
        functools.partial(kernel, dims),
        out_shape=jax.ShapeDtypeStruct((c_cap,) + block, dtype),
        in_specs=[any_space] * 9,
        out_specs=any_space,
        scratch_shapes=[pltpu.VMEM(v.shape, v.dtype) for v in small]
        + [pltpu.VMEM((n_c,) + rows, dtype)] * 4
        + [
            pltpu.VMEM((n_r * kb,) + part, dtype),
            pltpu.VMEM((n_r * kb,) + part, dtype),
            pltpu.VMEM((n_r * per * kb,) + part, dtype),
            pltpu.VMEM((per, kb) + block, dtype),
            pltpu.VMEM((per, kb) + part, dtype),
            pltpu.VMEM((8, LANES), F32),
            pltpu.VMEM((n_x, 8, LANES), F32),
            pltpu.VMEM((2, n_y, 8, LANES), F32),
            pltpu.VMEM((2, n_r, 8, LANES), F32),
        ]
        + [
            space((8, width), kind)
            for _ in range(2)
            for space in (pltpu.VMEM, pltpu.SMEM)
            for kind in (jnp.int32, F32)
        ]
        + [pltpu.VMEM(tile, F32)]
        + [pltpu.VMEM((kb * n_c + 1,) + tile, dtype)] * 4
        + [pltpu.VMEM((4 * half_c,) + tile, F32)]
        + [pltpu.VMEM((12 * (half_c // 2),) + tile, dtype)] * 4
        + [pltpu.VMEM((4 * half_c,) + tile, dtype)] * 2
        + [pltpu.VMEM((2 * half_c,) + tile, dtype)] * 2
        + [
            pltpu.VMEM((c_cap,) + block, dtype),
            dma((7,)),
            dma((n_meta,)),
            dma((n_meta,)),
            dma((n_ring,)),
            dma((n_ring,)),
            dma((n_units + n_ring,)),
            dma((n_units + n_ring,)),
            dma((per,)),
            dma((per,)),
            dma((28,)),
            dma((28,)),
        ]
        + [dma((12,))] * 4
        + [dma((8,))] * 2
        + [dma((4,))] * 2
        + [dma((8,))]
        + [dma((7,))],
        compiler_params=pltpu.CompilerParams(
            collective_id=0, has_side_effects=True, vmem_limit_bytes=62 * 1024 * 1024
        ),
    )(
        a_blocks,
        b_blocks.reshape(per, kb, edge, edge),
        *small,
    )
    copies = 10
    return pl.pallas_call(
        hand_over,
        out_shape=jax.ShapeDtypeStruct(gathered.shape, dtype),
        in_specs=[any_space],
        out_specs=any_space,
        scratch_shapes=[pltpu.VMEM(gathered.shape, dtype), dma((copies,)), dma((copies,))],
        compiler_params=pltpu.CompilerParams(vmem_limit_bytes=62 * 1024 * 1024),
    )(gathered)


def hand_over(src, dst, held, in_sems, out_sems):
    copies = in_sems.shape[0]
    size = src.shape[0] // copies
    parts = [pl.ds(i * size, size) for i in range(copies)]
    reads = [pltpu.make_async_copy(src.at[p], held.at[p], in_sems.at[i]) for i, p in enumerate(parts)]
    writes = [pltpu.make_async_copy(held.at[p], dst.at[p], out_sems.at[i]) for i, p in enumerate(parts)]
    for one in reads:
        one.start()
    for read, write in zip(reads, writes):
        read.wait()
        write.start()
    for one in writes:
        one.wait()


def solution(mesh):
    return jax.shard_map(
        shards,
        mesh=mesh,
        in_specs=(
            P(("row", "col", "depth"), None, None),
            P(("row", "col", "depth")),
            P(("row", "col", "depth")),
            P(("row", "col", "depth")),
            P("row", "col", "depth", None, None, None),
            P("row", "col", "depth", None),
            P("row", "col", "depth", None),
            P(("row", "col", "depth")),
            P(("row", "col", "depth")),
        ),
        out_specs=P(("row", "col", "depth"), None, None),
        check_vma=False,
    )
```

```python
import functools

import jax
import jax.numpy as jnp
from jax import lax
from jax.experimental import pallas as pl
from jax.experimental.pallas import tpu as pltpu
from jax.sharding import PartitionSpec as P

MESH = pl.DeviceIdType.MESH
LANES = 128
ROW_KEY = 1024.0
F32 = jnp.float32


def iota(shape, dim):
    return lax.broadcasted_iota(jnp.int32, shape, dim)


def schedule(dims, kind, meta_x, meta_y, meta_z, tab_int, tab_scale):
    n_x, n_y, n_r, a_cap, per, kb, c_cap = dims
    n_a = n_y * a_cap
    n_g = n_r * per
    n_slots = n_x * c_cap
    eye = iota((a_cap, LANES), 0) == iota((a_cap, LANES), 1)
    lane = iota((n_a, LANES), 1)

    def column(which):
        parts = [
            jnp.sum(jnp.where(eye, meta_y[kind, c, which : which + 1, :], 0.0), axis=1, keepdims=True)
            for c in range(n_y)
        ]
        return jnp.concatenate(parts, axis=0)

    a_scale, a_rows, a_cols = column(0), column(1), column(2)
    group = a_cols.astype(jnp.int32) // n_x
    b_scale = jnp.zeros((n_a, LANES), F32)
    b_cols = jnp.zeros((n_a, LANES), F32)
    for g in range(n_g):
        here = group == g
        d, i = g // per, g % per
        b_scale = jnp.where(here, meta_z[kind, d, 3 + i : 4 + i, :], b_scale)
        b_cols = jnp.where(here, meta_z[kind, d, 5 + i : 6 + i, :], b_cols)
    device, inner = group // per, group % per
    slots, weights, b_ids, first_ids = [], [], [], []
    for t in range(kb):
        col = jnp.sum(jnp.where(lane == t, b_cols, 0.0), axis=1, keepdims=True)
        scale = jnp.sum(jnp.where(lane == t, b_scale, 0.0), axis=1, keepdims=True)
        key = a_rows * ROW_KEY + col
        found = jnp.zeros((n_a, LANES), F32)
        for e in range(n_x):
            hit = (key == meta_x[e, 7:8, :]) & (lane < c_cap)
            found = jnp.where(hit, (lane + (e * c_cap + 1)).astype(F32), found)
        slot = jnp.max(found, axis=1, keepdims=True)
        slots.append(jnp.where(slot > 0, slot - 1, float(n_slots)))
        weights.append(a_scale * scale)
        b_ids.append((group * kb + t).astype(F32))
        first_ids.append((device * kb + t).astype(F32))
    slot, weight = jnp.concatenate(slots, axis=0), jnp.concatenate(weights, axis=0)
    a_id = jnp.concatenate([iota((n_a, 1), 0).astype(F32)] * kb, axis=0)
    b_id, first_id = jnp.concatenate(b_ids, axis=0), jnp.concatenate(first_ids, axis=0)
    low = jnp.where(jnp.concatenate([inner] * kb, axis=0) == 0, weight, 0.0)
    n_p = kb * n_a
    width = tab_int.shape[1]
    place, lane = iota((n_p, width), 0), iota((n_p, width), 1)
    row_slot = jnp.sum(jnp.where(place == lane, slot, 0.0), axis=0, keepdims=True)
    row_slot = jnp.where(lane[:1] < n_p, row_slot, 1e6)
    earlier = (row_slot == slot) & (lane < place)
    before = (row_slot < slot) | earlier
    rank = jnp.sum(jnp.where(before, 1.0, 0.0), axis=1, keepdims=True)
    keep = jnp.where(jnp.sum(jnp.where(earlier, 1.0, 0.0), axis=1, keepdims=True) > 0, 1.0, 0.0)
    lane_f = lane.astype(F32)
    mine = rank == lane_f

    def ordered(values):
        return jnp.sum(jnp.where(mine, values, 0.0), axis=0, keepdims=True)

    last = jnp.sum(jnp.where(slot <= lane_f, 1.0, 0.0), axis=0, keepdims=True) - 1.0
    some = jnp.sum(jnp.where(slot == lane_f, 1.0, 0.0), axis=0, keepdims=True)
    last = jnp.where(some > 0, last, float(n_p))
    zero = jnp.zeros((1, width), F32)
    table = jnp.concatenate(
        [ordered(a_id), ordered(b_id), last, ordered(first_id), zero, zero, zero, zero], axis=0
    ).astype(jnp.int32)
    which = iota(table.shape, 0)
    top = jnp.where(which == 0, n_a - 1, jnp.where(which == 1, n_g * kb - 1, n_p))
    top = jnp.where(which == 3, n_r * kb - 1, top)
    tab_int[...] = jnp.clip(table, 0, top)
    tab_scale[...] = jnp.concatenate(
        [ordered(weight), ordered(keep), ordered(low), ordered(weight - low), zero, zero, zero, zero], axis=0
    )


def kernel(
    dims, a_hbm, b_hbm, *rest):
    small, (out_hbm,), scratch = rest[:7], rest[7:8], rest[8:]
    body(dims, a_hbm, b_hbm, small, out_hbm, scratch[:7], *scratch[7:])


def body(
    dims, a_hbm, b_hbm, small, out_hbm, tables,
    a_own0, a_own1, a_pair0, a_pair1, b_one, b_two, b_second, raw_own, raw_pair, meta, meta_x, meta_y, meta_z,
    tab_int1, tab_scale1, ids1, scales1, tab_int2, tab_scale2, ids2, scales2,
    acc, prod0, prod1, prod2, prod3, own_first,
    to_right, to_left, from_left, from_right, to_mirror, from_mirror, to_pair, from_pair, result,
    local_sem, meta_send, meta_recv, ring_send, ring_recv, core_send, core_recv, raw_send, raw_recv, a_send, a_recv,
    r_send, r_recv, l_send, l_recv, m_send, m_recv, p_send, p_recv, out_sem, small_sem,
):
    n_x, n_y, n_r, a_cap, per, kb, c_cap = dims
    n_z = n_r // 2
    n_g = n_r * per
    n_c = n_y * a_cap
    half = b_second.shape[2]
    quarter = half // 2
    a_own, a_pair = (a_own0, a_own1), (a_pair0, a_pair1)
    first_prod = ((prod0, prod1), (prod2, prod3))
    own_prod, pair_prod = (prod0, prod1), (prod2, prod3)
    row, col, dep = lax.axis_index("row"), lax.axis_index("col"), lax.axis_index("depth")
    z, core = row // 2, row % 2

    def at_z(step):
        return (lax.rem(z + step + n_z, n_z) * 2 + core, col, dep)

    def at_y(step):
        return (row, lax.rem(col + step + n_y, n_y), dep)

    def at_x(step):
        return (row, col, lax.rem(dep + step + n_x, n_x))

    sibling = (z * 2 + 1 - core, col, dep)
    d_pair, d_mirror, d_far = dep + 1 - 2 * (dep % 2), n_x - 1 - dep, lax.rem(dep + 2, n_x)
    pair, mirror = (row, col, d_pair), (row, col, d_mirror)
    side = ((dep + 1) // 2) % 2
    second_cols = pl.ds(half, half)
    low_lanes = iota((1, half), 1) < quarter

    local_raw = pltpu.make_async_copy(b_hbm, raw_own, local_sem.at[0])
    local_raw.start()
    loads = [pltpu.make_async_copy(src, dst, small_sem.at[i]) for i, (src, dst) in enumerate(zip(small, tables))]
    for made in loads:
        made.start()
    a_scale, a_rows, a_cols, b_scale, b_cols, c_rows, c_cols = tables

    meta[...] = jnp.zeros_like(meta)
    for made in loads:
        made.wait()
    meta[0:1, 0:a_cap] = a_scale[...]
    meta[1:2, 0:a_cap] = a_rows[...].astype(F32)
    meta[2:3, 0:a_cap] = a_cols[...].astype(F32)
    meta[3 : 3 + per, 0:kb] = b_scale[...]
    meta[5 : 5 + per, 0:kb] = b_cols[...].astype(F32)
    meta[7:8, 0:c_cap] = c_rows[...].astype(F32) * ROW_KEY + c_cols[...].astype(F32)

    barrier = pltpu.get_barrier_semaphore()
    partners = [sibling, at_z(1), at_z(-1)] + [at_y(j) for j in range(1, n_y)] + [at_x(j) for j in range(1, n_x)]
    for partner in partners:
        pl.semaphore_signal(barrier, inc=1, device_id=partner, device_id_type=MESH)
    local_raw.wait()

    def pack_first(refs, number):
        for t in range(kb):
            one, two = raw_own[0, t, :, 0:half].astype(F32), raw_own[1, t, :, 0:half].astype(F32)
            one = pltpu.roll(one, quarter, 1) if number else one
            two = two if number else pltpu.roll(two, quarter, 1)
            refs[row * kb + t] = jnp.where(low_lanes, one, two).astype(refs.dtype)

    pack_first(b_one, 0)
    pl.semaphore_wait(barrier, len(partners))

    sends = []

    def copy(src, dst, send, recv, device):
        return pltpu.make_async_remote_copy(
            src_ref=src, dst_ref=dst, send_sem=send, recv_sem=recv, device_id=device, device_id_type=MESH
        )

    def push(src, dst, send, recv, device):
        made = copy(src, dst, send, recv, device)
        made.start()
        sends.append(made)

    def pulled(dst, send, recv):
        copy(dst, dst, send, recv, sibling).wait_recv()

    count = 0
    meta_waits = []
    for j in range(1, n_y):
        push(meta, meta_y.at[0, col], meta_send.at[count], meta_recv.at[count], at_y(j))
        meta_waits.append((meta_y.at[0, lax.rem(col - j + n_y, n_y)], count))
        count += 1
    for j in range(1, n_x):
        push(meta, meta_x.at[dep], meta_send.at[count], meta_recv.at[count], at_x(j))
        meta_waits.append((meta_x.at[lax.rem(dep - j + n_x, n_x)], count))
        count += 1
    push(meta, meta_z.at[0, row], meta_send.at[count], meta_recv.at[count], sibling)
    meta_waits.append((meta_z.at[0, z * 2 + 1 - core], count))
    count += 1
    hops_up, hops_down = n_z // 2, (n_z - 1) // 2
    ring_meta = count
    push(meta, meta_z.at[0, row], meta_send.at[count], meta_recv.at[count], at_z(1))
    push(meta, meta_z.at[0, row], meta_send.at[count + 1], meta_recv.at[count + 1], at_z(-1))
    count += 2 * hops_up
    core_meta = count
    count += 2 * hops_up
    pair_meta = count

    up, down = at_z(1), at_z(-1)
    units = [(b_one, kb, t, 1, t // 2) for t in range(kb)]
    units += [(b_two, kb, t, 1, 1 - t // 2) for t in range(kb)]
    units += [(b_second, per * kb, inner * kb, kb, inner) for inner in range(per)]
    n_u = len(units)
    unit_one, unit_two = list(range(kb)), list(range(kb, 2 * kb))
    unit_second = list(range(2 * kb, 2 * kb + per))

    def b_unit(origin_z, origin_core, unit):
        refs, each, first, size, _ = units[unit]
        return refs.at[pl.ds((origin_z * 2 + origin_core) * each + first, size)]

    def a_part(refs, origin, first):
        return refs.at[pl.ds(origin * a_cap + first, a_cap // 2)]

    def ring_slot(direction, step, unit):
        return (direction * hops_up + step) * n_u + unit

    def hops(direction, unit):
        return hops_up if units[unit][4] == direction else hops_down

    def send_first(src, unit):
        for direction, device in ((0, up), (1, down)):
            index = ring_slot(direction, 0, unit)
            push(src, b_unit(z, core, unit), ring_send.at[index], ring_recv.at[index], device)
        push(src, b_unit(z, core, unit), core_send.at[unit], core_recv.at[unit], sibling)

    for unit in unit_one:
        send_first(b_unit(z, core, unit), unit)
    for inner in range(per):
        push(b_hbm.at[inner, :, :, second_cols], raw_pair.at[inner], raw_send.at[inner], raw_recv.at[inner], pair)

    mid = a_cap // 2
    y_up, y_down = at_y(1), at_y(-1)
    left, right, across = at_y(-1)[1], at_y(1)[1], at_y(2)[1]

    def a_rows_of(rr, first):
        return a_hbm.at[pl.ds(first, mid), pl.ds(rr * half, half)]

    def send_own_a(rr):
        for first, slot, device in ((0, 0, y_up), (mid, 3, y_down), (mid, 1, y_up), (0, 4, y_down)):
            index = rr * 14 + slot
            push(a_rows_of(rr, first), a_part(a_own[rr], col, first), a_send.at[index], a_recv.at[index], device)

    def send_raw_a(rr):
        for number in range(2):
            first, index = number * mid, rr * 14 + 12 + number
            push(a_rows_of(rr, first), a_part(a_pair[rr], col, first), a_send.at[index], a_recv.at[index], pair)

    send_own_a(0)
    send_raw_a(0)
    local = [
        pltpu.make_async_copy(
            a_hbm.at[:, pl.ds(rr * half, half)], a_own[rr].at[pl.ds(col * a_cap, a_cap)], local_sem.at[1 + rr]
        )
        for rr in range(2)
    ]
    for made in local:
        made.start()
    meta_x[dep] = meta[...]
    meta_y[0, col] = meta[...]
    meta_z[0, row] = meta[...]

    def forward_meta(step):
        for direction, limit in ((0, hops_up), (1, hops_down)):
            if step >= limit:
                continue
            origin_z = lax.rem(z - step - 1 + n_z, n_z) if direction == 0 else lax.rem(z + step + 1, n_z)
            here = meta_z.at[0, origin_z * 2 + core]
            index = ring_meta + 2 * step + direction
            pulled(here, meta_send.at[index], meta_recv.at[index])
            if step + 1 < limit:
                push(here, here, meta_send.at[index + 2], meta_recv.at[index + 2], up if direction == 0 else down)
            index = core_meta + 2 * step + direction
            push(here, here, meta_send.at[index], meta_recv.at[index], sibling)
            meta_waits.append((meta_z.at[0, origin_z * 2 + 1 - core], index))

    def pair_tables():
        for here, index in meta_waits:
            pulled(here, meta_send.at[index], meta_recv.at[index])
        push(meta_y.at[0], meta_y.at[1], meta_send.at[pair_meta], meta_recv.at[pair_meta], pair)
        push(meta_z.at[0], meta_z.at[1], meta_send.at[pair_meta + 1], meta_recv.at[pair_meta + 1], pair)

    core_waits = [[(b_unit(z, 1 - core, unit), unit)] for unit in range(n_u)]

    def pack(inner):
        pulled(raw_pair.at[inner], raw_send.at[inner], raw_recv.at[inner])
        base = (row * per + inner) * kb
        for t in range(kb):
            mine, other = raw_own[inner, t, :, half : 2 * half].astype(F32), raw_pair[inner, t].astype(F32)
            mine = jnp.where(side == 0, mine, pltpu.roll(mine, quarter, 1))
            other = jnp.where(side == 0, pltpu.roll(other, quarter, 1), other)
            b_second[base + t] = jnp.where(low_lanes, mine, other).astype(b_second.dtype)

    def forward_b(step, unit):
        for direction in range(2):
            limit = hops(direction, unit)
            if step >= limit:
                continue
            origin_z = lax.rem(z - step - 1 + n_z, n_z) if direction == 0 else lax.rem(z + step + 1, n_z)
            here = b_unit(origin_z, core, unit)
            index = ring_slot(direction, step, unit)
            pulled(here, ring_send.at[index], ring_recv.at[index])
            if step + 1 < limit:
                index = ring_slot(direction, step + 1, unit)
                push(here, here, ring_send.at[index], ring_recv.at[index], up if direction == 0 else down)
            index = n_u + ring_slot(direction, step, unit)
            push(here, here, core_send.at[index], core_recv.at[index], sibling)
            core_waits[unit].append((b_unit(origin_z, 1 - core, unit), index))

    def arrived(refs, rr, origin, first, slot):
        here, index = a_part(refs[rr], origin, first), rr * 14 + slot
        pulled(here, a_send.at[index], a_recv.at[index])
        return here

    def hand_on(here, rr, slot, device):
        index = rr * 14 + slot
        push(here, here, a_send.at[index], a_recv.at[index], device)

    def across_a(refs, rr, base):
        hand_on(arrived(refs, rr, left, 0, base), rr, base + 2, y_up)
        hand_on(arrived(refs, rr, right, mid, base + 3), rr, base + 5, y_down)

    def rest_a(refs, rr, base):
        arrived(refs, rr, left, mid, base + 1)
        arrived(refs, rr, right, 0, base + 4)
        arrived(refs, rr, across, 0, base + 2)
        arrived(refs, rr, across, mid, base + 5)

    def spread_pair_a(rr):
        low_a, high_a = arrived(a_pair, rr, col, 0, 12), arrived(a_pair, rr, col, mid, 13)
        hand_on(low_a, rr, 6, y_up)
        hand_on(high_a, rr, 9, y_down)
        hand_on(high_a, rr, 7, y_up)
        hand_on(low_a, rr, 10, y_down)

    def finish(unit):
        for here, index in core_waits[unit]:
            pulled(here, core_send.at[index], core_recv.at[index])

    def plan(kind, tab_int, tab_scale, ids, scales, sem):
        schedule(dims, kind, meta_x, meta_y, meta_z, tab_int, tab_scale)
        made = [
            pltpu.make_async_copy(tab_int, ids, local_sem.at[sem]),
            pltpu.make_async_copy(tab_scale, scales, local_sem.at[sem + 1]),
        ]
        for one in made:
            one.start()
        return made

    def bounded(index, size):
        return jnp.clip(index, 0, size - 1)

    def multiply(a_refs, b_refs, ids, scales, prod, split):
        n_p = kb * n_c
        acc[...] = jnp.zeros_like(acc)
        prod[n_p] = jnp.zeros(prod.shape[1:], prod.dtype)

        @pl.loop(0, n_p, unroll=32)
        def _(j):
            left_block = a_refs[bounded(ids[0, j], n_c)]
            right_block = b_refs[bounded(ids[3 if split else 1, j], b_refs.shape[0])]
            product = jnp.dot(left_block, right_block, preferred_element_type=F32)
            weight = jnp.where(low_lanes, scales[2, j], scales[3, j]) if split else scales[0, j]
            total = acc[...] * scales[1, j] + product * weight
            acc[...] = total
            prod[j] = total.astype(prod.dtype)

    def folded(mine, other, dest, u, v):
        def take(which, index):
            prod, ids = which
            return prod[bounded(ids[2, dest * c_cap + index], prod.shape[0])].astype(F32)

        straight = jnp.where(low_lanes, take(mine, u), take(other, v))
        crossed = jnp.where(low_lanes, take(mine, v), take(other, u))
        return straight + pltpu.roll(crossed, quarter, 1)

    half_c = c_cap // 2
    pairs = half_c // 2
    x_up, x_down = at_x(1), at_x(-1)
    d_right, d_left = x_up[2], x_down[2]
    dtype = result.dtype

    def first_block(tile, dest, base, i):
        both = (first_prod[tile // 2][tile % 2], ids1)
        return folded(both, both, dest, base + i, base + pairs + i)

    def part(refs, tile, stage):
        return refs.at[pl.ds((tile * 3 + stage) * pairs, pairs)]

    def send_right(tile, stage):
        index = tile * 3 + stage
        return copy(part(to_right, tile, stage), part(from_left, tile, stage), r_send.at[index], r_recv.at[index], x_up)

    def send_left(tile, stage):
        index = tile * 3 + stage
        return copy(part(to_left, tile, stage), part(from_right, tile, stage), l_send.at[index], l_recv.at[index], x_down)

    def wait_left(tile, stage):
        here, index = part(from_left, tile, stage), tile * 3 + stage
        copy(here, here, r_send.at[index], r_recv.at[index], x_up).wait_recv()

    def wait_right(tile, stage):
        here, index = part(from_right, tile, stage), tile * 3 + stage
        copy(here, here, l_send.at[index], l_recv.at[index], x_down).wait_recv()

    def first_sends(tile):
        at = tile * 3 * pairs

        @pl.loop(0, pairs, unroll=pairs)
        def _(i):
            to_right[at + i] = first_block(tile, d_far, 0, i).astype(dtype)

        send_right(tile, 0).start()

        @pl.loop(0, pairs, unroll=pairs)
        def _(i):
            to_left[at + i] = first_block(tile, d_far, half_c, i).astype(dtype)

        send_left(tile, 0).start()

        @pl.loop(0, pairs, unroll=pairs)
        def _(i):
            to_right[at + pairs + i] = first_block(tile, d_right, half_c, i).astype(dtype)

        send_right(tile, 1).start()

        @pl.loop(0, pairs, unroll=pairs)
        def _(i):
            to_left[at + pairs + i] = first_block(tile, d_left, 0, i).astype(dtype)

        send_left(tile, 1).start()

    def pass_sums(tile):
        at = tile * 3 * pairs
        wait_left(tile, 0)

        @pl.loop(0, pairs, unroll=pairs)
        def _(i):
            total = first_block(tile, d_right, 0, i) + from_left[at + i].astype(F32)
            to_right[at + 2 * pairs + i] = total.astype(dtype)

        send_right(tile, 2).start()
        wait_right(tile, 0)

        @pl.loop(0, pairs, unroll=pairs)
        def _(i):
            total = first_block(tile, d_left, half_c, i) + from_right[at + i].astype(F32)
            to_left[at + 2 * pairs + i] = total.astype(dtype)

        send_left(tile, 2).start()

    def keep_own(tile):
        @pl.loop(0, pairs, unroll=pairs)
        def _(i):
            own_first[tile * half_c + i] = first_block(tile, dep, 0, i)
            own_first[tile * half_c + pairs + i] = first_block(tile, dep, half_c, i)

    def first_results(rr):
        tiles = (rr, 2 + rr)
        rows = slice(rr * half, (rr + 1) * half)
        for tile in tiles:
            for stage in (1, 2):
                wait_right(tile, stage)
                wait_left(tile, stage)
        for base, kept, left_stage, right_stage in ((0, 0, 2, 1), (half_c, pairs, 1, 2)):

            @pl.loop(0, pairs, unroll=pairs)
            def _(i):
                one, two = [
                    own_first[tile * half_c + kept + i]
                    + from_left[(tile * 3 + left_stage) * pairs + i].astype(F32)
                    + from_right[(tile * 3 + right_stage) * pairs + i].astype(F32)
                    for tile in tiles
                ]
                result[base + i, rows, 0:half] = jnp.where(low_lanes, one, pltpu.roll(two, quarter, 1)).astype(dtype)
                result[base + pairs + i, rows, 0:half] = jnp.where(
                    low_lanes, pltpu.roll(one, quarter, 1), two
                ).astype(dtype)

    def packed(rr, dest, u):
        return folded((own_prod[rr], ids1), (pair_prod[rr], ids2), dest, u, half_c + u)

    def second_part(refs, rr, stage, k, stages):
        return refs.at[pl.ds((rr * stages + stage) * half_c + k * pairs, pairs)]

    def send_mirror(rr, stage, k):
        index = (rr * 2 + stage) * 2 + k
        return copy(
            second_part(to_mirror, rr, stage, k, 2), second_part(from_mirror, rr, stage, k, 2),
            m_send.at[index], m_recv.at[index], mirror,
        )

    def send_pair(rr, k):
        index = rr * 2 + k
        return copy(
            second_part(to_pair, rr, 0, k, 1), second_part(from_pair, rr, 0, k, 1),
            p_send.at[index], p_recv.at[index], pair,
        )

    def second_sends(rr, stage):
        dest = (d_far, d_mirror)[stage]
        for k in range(2):

            @pl.loop(0, pairs, unroll=pairs)
            def _(i):
                u = k * pairs + i
                to_mirror[(rr * 2 + stage) * half_c + u] = packed(rr, dest, u).astype(dtype)

            send_mirror(rr, stage, k).start()

    def second_sums(rr):
        for k in range(2):
            send_mirror(rr, 0, k).wait_recv()

            @pl.loop(0, pairs, unroll=pairs)
            def _(i):
                u = k * pairs + i
                total = packed(rr, d_pair, u) + from_mirror[rr * 2 * half_c + u].astype(F32)
                to_pair[rr * half_c + u] = total.astype(dtype)

            send_pair(rr, k).start()

    def write(rr, k):
        rows = pl.ds(rr * half, half)
        return [
            pltpu.make_async_copy(
                result.at[pl.ds(first + k * pairs, pairs), rows], out_hbm.at[pl.ds(first + k * pairs, pairs), rows],
                out_sem.at[(rr * 2 + k) * 2 + number],
            )
            for number, first in enumerate((0, half_c))
        ]

    def second_results(rr):
        rows = slice(rr * half, (rr + 1) * half)
        for k in range(2):
            send_pair(rr, k).wait_recv()
            send_mirror(rr, 1, k).wait_recv()

            @pl.loop(0, pairs, unroll=pairs)
            def _(i):
                u = k * pairs + i
                mine = packed(rr, dep, u) + from_mirror[(rr * 2 + 1) * half_c + u].astype(F32)
                other = from_pair[rr * half_c + u].astype(F32)
                low = jnp.where(side == 0, mine, other)
                high = jnp.where(side == 0, other, mine)
                result[u, rows, half : 2 * half] = jnp.where(low_lanes, low, pltpu.roll(high, quarter, 1)).astype(dtype)
                result[half_c + u, rows, half : 2 * half] = jnp.where(
                    low_lanes, pltpu.roll(low, quarter, 1), high
                ).astype(dtype)

            for made in write(rr, k):
                made.start()

    forward_meta(0)
    pack_first(b_two, 1)
    forward_b(0, unit_one[0])
    forward_b(0, unit_one[1])
    forward_b(0, unit_one[2])
    send_first(b_unit(z, core, unit_two[0]), unit_two[0])
    send_first(b_unit(z, core, unit_two[1]), unit_two[1])
    forward_b(1, unit_one[1])
    forward_meta(1)
    pack(0)
    forward_b(1, unit_one[2])
    across_a(a_own, 0, 0)
    forward_b(1, unit_one[0])
    forward_b(0, unit_two[0])
    forward_meta(2)
    send_first(b_unit(z, core, unit_two[2]), unit_two[2])
    pack(1)
    forward_b(2, unit_one[2])
    forward_b(2, unit_one[1])
    send_own_a(1)
    forward_b(0, unit_two[1])
    forward_b(1, unit_two[0])
    forward_b(2, unit_one[0])
    forward_meta(3)
    forward_b(0, unit_two[2])
    send_raw_a(1)
    rest_a(a_own, 0, 0)
    send_first(b_unit(z, core, unit_second[0]), unit_second[0])
    pair_tables()
    forward_b(3, unit_one[2])
    forward_b(1, unit_two[1])
    forward_b(3, unit_one[1])
    finish(unit_one[2])
    table1 = plan(0, tab_int1, tab_scale1, ids1, scales1, 3)
    finish(unit_one[1])
    across_a(a_own, 1, 0)
    forward_b(3, unit_one[0])
    forward_b(1, unit_two[2])
    for made in table1 + local:
        made.wait()
    spread_pair_a(0)
    finish(unit_one[0])
    forward_b(2, unit_two[0])
    send_first(b_unit(z, core, unit_second[1]), unit_second[1])
    multiply(a_own[0], b_one, ids1, scales1, prod0, True)
    first_sends(0)
    forward_b(2, unit_two[1])
    forward_b(2, unit_two[2])
    forward_b(0, unit_second[0])
    rest_a(a_own, 1, 0)
    multiply(a_own[1], b_one, ids1, scales1, prod1, True)
    first_sends(1)
    forward_b(0, unit_second[1])
    spread_pair_a(1)
    forward_b(3, unit_two[1])
    pass_sums(0)
    pulled(meta_y.at[1], meta_send.at[pair_meta], meta_recv.at[pair_meta])
    pulled(meta_z.at[1], meta_send.at[pair_meta + 1], meta_recv.at[pair_meta + 1])
    table2 = plan(1, tab_int2, tab_scale2, ids2, scales2, 5)
    forward_b(3, unit_two[0])
    forward_b(1, unit_second[0])
    forward_b(3, unit_two[2])
    finish(unit_two[0])
    pass_sums(1)
    finish(unit_two[2])
    finish(unit_two[1])
    forward_b(1, unit_second[1])
    multiply(a_own[0], b_two, ids1, scales1, prod2, True)
    first_sends(2)
    forward_b(2, unit_second[0])
    across_a(a_pair, 1, 6)
    multiply(a_own[1], b_two, ids1, scales1, prod3, True)
    forward_b(2, unit_second[1])
    for made in table2:
        made.wait()
    keep_own(0)
    first_sends(3)
    pass_sums(2)
    forward_b(3, unit_second[0])
    keep_own(2)
    keep_own(1)
    rest_a(a_pair, 1, 6)
    finish(unit_second[0])
    across_a(a_pair, 0, 6)
    forward_b(3, unit_second[1])
    pass_sums(3)
    finish(unit_second[1])
    multiply(a_own[1], b_second, ids1, scales1, prod1, False)
    keep_own(3)
    multiply(a_pair[1], b_second, ids2, scales2, prod3, False)
    second_sends(1, 0)
    multiply(a_own[0], b_second, ids1, scales1, prod0, False)
    second_sends(1, 1)
    first_results(0)
    second_sums(1)
    rest_a(a_pair, 0, 6)
    multiply(a_pair[0], b_second, ids2, scales2, prod2, False)
    second_sends(0, 0)
    second_sends(0, 1)
    first_results(1)
    second_results(1)
    second_sums(0)
    second_results(0)

    for rr in range(2):
        for k in range(2):
            for made in write(rr, k):
                made.wait()
            send_pair(rr, k).wait_send()
            for stage in range(2):
                send_mirror(rr, stage, k).wait_send()
    for tile in range(4):
        for stage in range(3):
            send_right(tile, stage).wait_send()
            send_left(tile, stage).wait_send()

    for made in sends:
        made.wait_send()


def shards(a_blocks, a_scale, a_rows, a_cols, b_blocks, b_scale, b_cols, c_rows, c_cols):
    edge = a_blocks.shape[1]
    half = edge // 2
    a_cap, c_cap = a_blocks.shape[0], c_rows.shape[0]
    per, kb = b_blocks.shape[0], b_blocks.shape[3]
    n_r, n_y, n_x = lax.axis_size("row"), lax.axis_size("col"), lax.axis_size("depth")
    dims = (n_x, n_y, n_r, a_cap, per, kb, c_cap)
    n_c = n_y * a_cap
    half_c = c_cap // 2

    width = -(-kb * n_c // LANES) * LANES

    dtype = a_blocks.dtype
    block, part = (edge, edge), (edge, half)
    dma = pltpu.SemaphoreType.DMA
    hops = n_r // 4
    n_meta = (n_y - 1) + (n_x - 1) + 1 + 4 * hops + 2
    n_units = 2 * kb + per
    n_ring = 2 * hops * n_units
    rows = (half, edge)
    tile = (half, half)
    any_space = pl.BlockSpec(memory_space=pl.ANY)
    small = [v.reshape(1, a_cap) for v in (a_scale, a_rows, a_cols)]
    small += [v.reshape(per, kb) for v in (b_scale, b_cols)]
    small += [v.reshape(1, c_cap) for v in (c_rows, c_cols)]
    gathered = pl.pallas_call(
        functools.partial(kernel, dims),
        out_shape=jax.ShapeDtypeStruct((c_cap,) + block, dtype),
        in_specs=[any_space] * 9,
        out_specs=any_space,
        scratch_shapes=[pltpu.VMEM(v.shape, v.dtype) for v in small]
        + [pltpu.VMEM((n_c,) + rows, dtype)] * 4
        + [
            pltpu.VMEM((n_r * kb,) + part, dtype),
            pltpu.VMEM((n_r * kb,) + part, dtype),
            pltpu.VMEM((n_r * per * kb,) + part, dtype),
            pltpu.VMEM((per, kb) + block, dtype),
            pltpu.VMEM((per, kb) + part, dtype),
            pltpu.VMEM((8, LANES), F32),
            pltpu.VMEM((n_x, 8, LANES), F32),
            pltpu.VMEM((2, n_y, 8, LANES), F32),
            pltpu.VMEM((2, n_r, 8, LANES), F32),
        ]
        + [
            space((8, width), kind)
            for _ in range(2)
            for space in (pltpu.VMEM, pltpu.SMEM)
            for kind in (jnp.int32, F32)
        ]
        + [pltpu.VMEM(tile, F32)]
        + [pltpu.VMEM((kb * n_c + 1,) + tile, dtype)] * 4
        + [pltpu.VMEM((4 * half_c,) + tile, F32)]
        + [pltpu.VMEM((12 * (half_c // 2),) + tile, dtype)] * 4
        + [pltpu.VMEM((4 * half_c,) + tile, dtype)] * 2
        + [pltpu.VMEM((2 * half_c,) + tile, dtype)] * 2
        + [
            pltpu.VMEM((c_cap,) + block, dtype),
            dma((7,)),
            dma((n_meta,)),
            dma((n_meta,)),
            dma((n_ring,)),
            dma((n_ring,)),
            dma((n_units + n_ring,)),
            dma((n_units + n_ring,)),
            dma((per,)),
            dma((per,)),
            dma((28,)),
            dma((28,)),
        ]
        + [dma((12,))] * 4
        + [dma((8,))] * 2
        + [dma((4,))] * 2
        + [dma((8,))]
        + [dma((7,))],
        compiler_params=pltpu.CompilerParams(
            collective_id=0, has_side_effects=True, vmem_limit_bytes=62 * 1024 * 1024
        ),
    )(
        a_blocks,
        b_blocks.reshape(per, kb, edge, edge),
        *small,
    )
    copies = 10
    return pl.pallas_call(
        hand_over,
        out_shape=jax.ShapeDtypeStruct(gathered.shape, dtype),
        in_specs=[any_space],
        out_specs=any_space,
        scratch_shapes=[pltpu.VMEM(gathered.shape, dtype), dma((copies,)), dma((copies,))],
        compiler_params=pltpu.CompilerParams(vmem_limit_bytes=62 * 1024 * 1024),
    )(gathered)


def hand_over(src, dst, held, in_sems, out_sems):
    copies = in_sems.shape[0]
    size = src.shape[0] // copies
    parts = [pl.ds(i * size, size) for i in range(copies)]
    reads = [pltpu.make_async_copy(src.at[p], held.at[p], in_sems.at[i]) for i, p in enumerate(parts)]
    writes = [pltpu.make_async_copy(held.at[p], dst.at[p], out_sems.at[i]) for i, p in enumerate(parts)]
    for one in reads:
        one.start()
    for read, write in zip(reads, writes):
        read.wait()
        write.start()
    for one in writes:
        one.wait()


def solution(mesh):
    return jax.shard_map(
        shards,
        mesh=mesh,
        in_specs=(
            P(("row", "col", "depth"), None, None),
            P(("row", "col", "depth")),
            P(("row", "col", "depth")),
            P(("row", "col", "depth")),
            P("row", "col", "depth", None, None, None),
            P("row", "col", "depth", None),
            P("row", "col", "depth", None),
            P(("row", "col", "depth")),
            P(("row", "col", "depth")),
        ),
        out_specs=P(("row", "col", "depth"), None, None),
        check_vma=False,
    )
```
